128 devices in a mesh: region: 16 (over y, x), tm: 8 (over z, core).
Axes of the slice: x: 4, y: 4, z: 4, core: 2. Of those that a mesh axis runs over, the one named last changes fastest.
Arguments:
- jacobian: bfloat16 [98304, 2048], P(('region', 'tm')), may hold values from -0.375 to 0.375
- foot_block: int32 [98304], P(('region', 'tm')), may hold values from 0 to 127, as said below
- foot_time: int32 [98304], P(('region', 'tm')), may hold values from 0 to 432, as said below
- obs_weight: bfloat16 [98304], P(('region', 'tm')), may hold values from 0.29882812 to 3
- misfit: bfloat16 [98304], P(('region', 'tm')), may hold values from -6 to 6
- kept_list: int32 [65536], P(('region', 'tm')), may hold values from 0 to 767, as said below
- kept_count: int32 [128], P(('region', 'tm')), may hold values from 256 to 512, as said below
- prior_std: float32 [448, 128, 128], P('tm', 'region'), may hold values from 0.4 to 11
- time_factor: float32 [448, 448], replicated, may hold values from -0.3 to 1.3
Outputs:
- solution: float32 [448, 128, 128], P('tm', 'region')
- residual: float32 [448, 128, 128], P('tm', 'region')
The draws below stay inside these ranges and needn't reach their ends.
Inputs may be any that keep to these rules, and one draw needn't show every extreme that they name: `kept_list`: the 512 entries of one device are distinct row numbers within that device's own 768 rows. A device keeps the rows named by the first kept_count entries of its list. Region block of the footprint; the block is owned by the region index foot_block // 8. A footprint covers steps foot_time to foot_time + 15, all in the time window foot_time // 56: foot_time % 56 <= 40. Among the kept rows of one device, at most 6 have footprints owned by any one device (region index foot_block // 8, time index foot_time // 56); in every draw some owning device gets exactly 6 kept rows from every device.
All inputs are finite; a program needn't handle non-finite values.
Results may differ from the reference program's by a relative error of at most 0.0004.
Values may be sent and summed in bfloat16 or wider, within the bound.
A program may use at most 128 MiB of HBM per device.

```python
import math
import jax
import jax.numpy as jnp
from jax import lax

CELLS = 128
REG_DEV = 8
TDEV = 56
LAG = 16
KEEP = 512
ITERS = 2
POOL = 768
CAP = 6
REGIONS = 128
NT = 448
N_REGION = 16
N_TM = 8


def sounding_plan(key):
    key = jax.random.fold_in(key, 31)
    devices = N_REGION * N_TM
    capacity = CAP
    key_heavy, key_count, key_full, key_low, key_rows = jax.random.split(key, 5)
    heavy = jax.random.randint(key_heavy, (), 0, devices)

    def one_device(sub):
        parts = jax.random.split(sub, 8)
        order = jax.random.permutation(parts[0], POOL)[:KEEP].astype(jnp.int32)
        spots = jax.random.permutation(parts[1], (devices - 1) * capacity)[:KEEP - capacity].astype(jnp.int32)
        others = spots // capacity
        others = others + (others >= heavy).astype(jnp.int32)
        target = jnp.concatenate([jnp.full((capacity,), heavy, jnp.int32), others])
        shuffle = jax.random.permutation(parts[2], KEEP // 2)
        target = jnp.concatenate([target[:KEEP // 2][shuffle], target[KEEP // 2:]])
        inside = jax.random.randint(parts[3], (KEEP,), 0, REG_DEV)
        offset = jax.random.randint(parts[4], (KEEP,), 0, TDEV - LAG + 1)
        blocks = target // N_TM * REG_DEV + inside
        starts = target % N_TM * TDEV + offset
        pool_blocks = jax.random.randint(parts[5], (POOL,), 0, REGIONS)
        pool_starts = jax.random.randint(parts[6], (POOL,), 0, N_TM) * TDEV + jax.random.randint(parts[7], (POOL,), 0, TDEV - LAG + 1)
        pool_blocks = pool_blocks.at[order].set(blocks)
        pool_starts = pool_starts.at[order].set(starts)
        return (order, pool_blocks.astype(jnp.int32), pool_starts.astype(jnp.int32))
    lists, blocks, starts = jax.vmap(one_device)(jax.random.split(key_rows, devices))
    counts = jax.random.randint(key_count, (devices,), KEEP // 2, KEEP + 1)
    full_at = jax.random.randint(key_full, (), 0, devices)
    low_at = (full_at + 1 + jax.random.randint(key_low, (), 0, devices - 1)) % devices
    counts = counts.at[full_at].set(KEEP).at[low_at].set(KEEP // 2)
    return (lists.reshape(-1), counts.astype(jnp.int32), blocks.reshape(-1), starts.reshape(-1))


def draw_kept_list(key, part):
    return sounding_plan(key)[0]


def draw_kept_count(key, part):
    return sounding_plan(key)[1]


def draw_foot_block(key, part):
    return sounding_plan(key)[2]


def draw_foot_time(key, part):
    return sounding_plan(key)[3]


def draw_prior_std(key, part):
    key = jax.random.fold_in(key, 57)
    ramp = 3.0 ** (jnp.arange(REGIONS, dtype=jnp.float32) / REGIONS)
    shape = (NT, REGIONS, CELLS)
    base = jnp.exp(jax.random.uniform(key, shape, jnp.float32, math.log(0.4), math.log(1.2)))
    return base * ramp[None, :, None]


def draw_time_factor(key, part):
    key = jax.random.fold_in(key, 83)
    ident = (jnp.arange(NT)[:, None] == jnp.arange(NT)[None, :]).astype(jnp.float32)
    noise = jnp.clip(jax.random.normal(key, (NT, NT), jnp.float32), -3.0, 3.0)
    return ident + 0.5 / math.sqrt(NT) * noise


def block_scale(stream_key, dims, shards, low, high):
    def one(position, shards_of):
        steps = jax.random.uniform(jax.random.fold_in(jax.random.fold_in(stream_key, 6), position), (shards_of,), jnp.float32, low / len(shards), high / len(shards))
        return jnp.repeat(jnp.exp(steps), dims[position] // shards_of).reshape((-1,) + (1,) * (len(dims) - position - 1))

    loudness = one(*shards[0])
    for cut in shards[1:]:
        loudness = loudness * one(*cut)
    return loudness


def centred(own_key, shape, deviation, reach, shards=(), held_as=jnp.bfloat16):
    values = jax.random.normal(own_key, shape, jnp.float32) * deviation
    if len(shards) > 0:
        values = block_scale(own_key, shape, shards, -0.22, 0.18) * values
    return jnp.clip(values, min=-reach, max=reach).astype(held_as)


def setup_inputs(seed: int = 0) -> dict:
    keys = jax.random.split(jax.random.key(seed), 10)
    return {
        "jacobian": centred(keys[0], (N_REGION * N_TM * POOL, LAG * CELLS), (LAG * CELLS // 8) ** -0.5, 0.375, ((0, 128),)),
        "foot_block": draw_foot_block(jax.random.fold_in(keys[9], 71), 0),
        "foot_time": draw_foot_time(jax.random.fold_in(keys[9], 71), 0),
        "obs_weight": jnp.clip(jnp.exp(math.log(3.0) - 2.306499 * jax.random.uniform(keys[3], (N_REGION * N_TM * POOL,), jnp.float32) ** block_scale(keys[3], (N_REGION * N_TM * POOL,), ((0, 128),), -0.2, 0.2)), 0.29882812, 3.0).astype(jnp.bfloat16),
        "misfit": centred(keys[4], (N_REGION * N_TM * POOL,), 1.0, 6.0, ((0, 128),)),
        "kept_list": draw_kept_list(jax.random.fold_in(keys[9], 71), 0),
        "kept_count": draw_kept_count(jax.random.fold_in(keys[9], 71), 0),
        "prior_std": draw_prior_std(jax.random.fold_in(keys[9], 71), 0),
        "time_factor": draw_time_factor(jax.random.fold_in(keys[9], 71), 0),
    }


def reference(jacobian, foot_block, foot_time, obs_weight, misfit, kept_list, kept_count, prior_std, time_factor):
    flat_shape = (NT * REGIONS, CELLS)
    offsets = jnp.arange(LAG, dtype=jnp.int32)

    def sounding_pass(field, with_field):
        flat = field.reshape(flat_shape)

        def visit(total, device):
            selected = lax.dynamic_slice_in_dim(kept_list, device * KEEP, KEEP, 0).astype(jnp.int32) + (device * POOL).astype(jnp.int32)
            shaped = jacobian[selected].astype(jnp.float32).reshape(KEEP, LAG, CELLS)
            index = (foot_time[selected][:, None].astype(jnp.int32) + offsets[None, :]) * REGIONS + foot_block[selected][:, None].astype(jnp.int32)
            kept_now = jnp.arange(KEEP, dtype=jnp.int32) < kept_count[device]
            weight = jnp.where(kept_now, obs_weight[selected].astype(jnp.float32), jnp.zeros((KEEP,), jnp.float32))
            if with_field:
                values = weight * jnp.sum(shaped * flat[index], axis=(1, 2))
            else:
                values = weight * misfit[selected].astype(jnp.float32)
            return total.at[index].add(shaped * values[:, None, None]), None

        total = lax.scan(visit, jnp.zeros(flat_shape, jnp.float32), jnp.arange(N_REGION * N_TM, dtype=jnp.int32))[0]
        return total.reshape(NT, REGIONS, CELLS)

    def lower(field):
        mixed = jnp.dot(time_factor, field.reshape(NT, REGIONS * CELLS), precision=lax.Precision.HIGHEST)
        return prior_std * mixed.reshape(NT, REGIONS, CELLS)

    def upper(field):
        mixed = jnp.dot(time_factor.T, (prior_std * field).reshape(NT, REGIONS * CELLS), precision=lax.Precision.HIGHEST)
        return mixed.reshape(NT, REGIONS, CELLS)

    def operator(field):
        return field + upper(sounding_pass(lower(field), True))

    rhs = upper(sounding_pass(prior_std, False))
    solution = jnp.zeros_like(rhs)
    residual = rhs
    direction = rhs
    norm_now = jnp.sum(residual * residual)
    for iteration in range(ITERS):
        image = operator(direction)
        alpha = norm_now / jnp.sum(direction * image)
        solution = solution + alpha * direction
        residual = residual - alpha * image
        norm_next = jnp.sum(residual * residual)
        direction = residual + (norm_next / norm_now) * direction
        norm_now = norm_next
    return solution, residual
```

```python
import functools

import jax
import jax.numpy as jnp
from jax import lax
from jax.experimental import pallas as pl
from jax.experimental.pallas import tpu as pltpu
from jax.sharding import PartitionSpec as P

MESH = pl.DeviceIdType.MESH
HIGH = lax.Precision.HIGHEST
F32 = jnp.float32
BF16 = jnp.bfloat16
I32 = jnp.int32

BATCHES = (
    ((0, 1), (1, 0)),
    ((0, 3), (3, 0)),
    ((1, 1), (3, 3)),
    ((1, 3), (3, 1)),
    ((1, 2), (2, 1)),
    ((3, 2), (2, 3)),
    ((0, 2), (2, 0)),
    ((2, 2), (0, 0)),
)
NT_DIMS = (((1,), (1,)), ((), ()))
TN_DIMS = (((0,), (0,)), ((), ()))


def iota(shape, axis):
    return lax.broadcasted_iota(I32, shape, axis)


def dot(a, b):
    return jnp.dot(a, b, preferred_element_type=F32)


def group_transpose(x):
    shape = x.shape
    sub, grp = iota(shape, 1), iota(shape, 2) >> 4
    for s in (1, 2, 4):
        sub_bit, lane_bit = (sub & s) != 0, (grp & s) != 0
        up = pltpu.roll(pltpu.roll(x, 8 - s, 1), 16 * s, 2)
        down = pltpu.roll(pltpu.roll(x, s, 1), 128 - 16 * s, 2)
        x = jnp.where(sub_bit == lane_bit, x, jnp.where(lane_bit, up, down))
    return x


def split(x):
    low = x - x.astype(BF16).astype(F32)
    return jnp.concatenate([x, low], axis=0).astype(BF16)


def kernel(
    jac, fb_row, ft_row, ft_col, w_row, y_row, klist, kcount, prior, factor,
    x_out, r_out,
    jp, place, order, xs, rbuf, msend, mrecv, jw,
    psend, sig, cov, key, wgt, wy, uval, ubuf, vec,
    ss, gs, scal, scal_in, osend, obuf, ptmp,
    s_sem, ms_sem, r_sem, m_sem, ps_sem, p_sem, us_sem, u_sem, cs_sem, c_sem, os_sem, o_sem, l_sem,
):
    r, m = lax.axis_index("region"), lax.axis_index("tm")
    y, x, z, c = r // 4, r % 4, m // 2, m % 2

    def region_at(dy, dx):
        return ((y + dy) % 4) * 4 + (x + dx) % 4

    def tm_at(d):
        return ((z + d // 2) % 4) * 2 + (c + d) % 2

    barrier = pltpu.get_barrier_semaphore()

    def greet(i, carry):
        o = i // 8
        pl.semaphore_signal(
            barrier, inc=1, device_id=(region_at(o // 4, o % 4), tm_at(i % 8)), device_id_type=MESH
        )
        return carry

    lax.fori_loop(1, 128, greet, 0)

    blocks, starts = fb_row[...], ft_row[...]
    window = (starts * 1171) >> 16
    offset = starts - 56 * window
    kept = jnp.sum(
        jnp.where((klist[...] == iota((512, 768), 1)) & (iota((512, 768), 0) < kcount[...]), 1.0, 0.0),
        axis=0, keepdims=True,
    )
    target = (blocks >> 3) * 8 + window
    chosen = jnp.where((iota((128, 768), 0) == target) & (kept > 0.5), 1.0, 0.0)
    before = jnp.where(iota((768, 768), 0) < iota((768, 768), 1), 1.0, 0.0).astype(BF16)
    rank = jnp.sum(chosen * dot(chosen.astype(BF16), before), axis=0, keepdims=True)
    slot = jnp.where(kept > 0.5, target * 6 + rank.astype(I32), -1)
    place[...] = jnp.where(iota((768, 768), 0) == slot, 1.0, 0.0).astype(BF16)

    row = iota((16, 768), 0)
    meta = jnp.where(row == 0, (blocks & 7).astype(F32), 0.0)
    meta = jnp.where(row == 1, offset.astype(F32), meta)
    meta = jnp.where(row == 2, w_row[...].astype(F32), meta)
    meta = jnp.where(row == 3, y_row[...].astype(F32), meta)
    meta = lax.dot_general(meta.astype(BF16), place[...], NT_DIMS, preferred_element_type=F32)
    lane = iota((1, 128), 1)
    for i in range(16):
        part = meta if i == 0 else pltpu.roll(meta, 768 - 48 * i, 1)
        part = part[:, :128]
        msend[i, 0:1, :] = jnp.where(
            lane < 64, part[0:1] * 64.0 + part[1:2], pltpu.roll(part[2:3], 64, 1)
        )
        msend[i, 1:2, :] = part[2:3] * part[3:4]

    ptmp[...] = group_transpose(prior[...])
    for i in range(8):
        psend[i] = ptmp[:, i, :]
    sig[m] = psend[m]

    def turn(i, carry):
        rows = pl.ds(pl.multiple_of(i * 16, 16), 16)
        start = ft_col[rows, :]
        rho = (start - 56 * ((start * 1171) >> 16)) & 15
        lanes = iota((16, 128), 1) >> 4
        parts = [jac[rows, l * 128 : (l + 1) * 128].astype(F32) for l in range(16)]
        for s in (1, 2, 4, 8):
            bit = jnp.broadcast_to((rho & s), (16, 128)) != 0
            parts = [jnp.where(bit, parts[(l - s) % 16], parts[l]) for l in range(16)]
        for half in range(2):
            v = parts[half * 8 : half * 8 + 8]
            for s in (1, 2, 4):
                bit = (lanes & s) != 0
                new = list(v)
                for k in range(8):
                    if k & s == 0:
                        new[k] = jnp.where(bit, pltpu.roll(v[k + s], 16 * s, 1), v[k])
                        new[k + s] = jnp.where(bit, v[k + s], pltpu.roll(v[k], 128 - 16 * s, 1))
                v = new
            for k in range(8):
                jp[k, rows, half * 128 : (half + 1) * 128] = v[k].astype(BF16)
        return carry

    lax.fori_loop(0, 48, turn, 0)

    def pick(i, carry):
        rows = dot(place[...], jp[i]).astype(BF16)
        xs[pl.ds(i * 16, 16)] = rows.reshape(16, 48, 256)
        return carry

    lax.fori_loop(0, 8, pick, 0)

    pl.semaphore_wait(barrier, 127)

    def send_prior(d, carry):
        t = tm_at(d)
        pltpu.make_async_remote_copy(
            src_ref=psend.at[t], dst_ref=sig.at[m], send_sem=ps_sem, recv_sem=p_sem,
            device_id=(r, t), device_id_type=MESH,
        ).start()
        return carry

    lax.fori_loop(1, 8, send_prior, 0)

    own = 7 * 16 + 8 + m
    local_rows = pltpu.make_async_copy(xs.at[m * 16 + r], rbuf.at[own], r_sem.at[7])
    local_meta = pltpu.make_async_copy(msend.at[r], mrecv.at[own], m_sem.at[7])
    local_rows.start()
    local_meta.start()
    for g in range(8):

        def send(d, carry, g=g, which=(0, 1)):
            t = tm_at(d)
            for k in which:
                to = region_at(*BATCHES[g][k])
                here = g * 16 + k * 8 + m
                pltpu.make_async_remote_copy(
                    src_ref=msend.at[to], dst_ref=mrecv.at[here], send_sem=ms_sem, recv_sem=m_sem.at[g],
                    device_id=(to, t), device_id_type=MESH,
                ).start()
                pltpu.make_async_remote_copy(
                    src_ref=xs.at[t * 16 + to], dst_ref=rbuf.at[here], send_sem=s_sem, recv_sem=r_sem.at[g],
                    device_id=(to, t), device_id_type=MESH,
                ).start()
            return carry

        if g < 7:
            lax.fori_loop(0, 8, send, 0)
        else:
            send(0, 0, which=(0,))
            lax.fori_loop(1, 8, send, 0)

    cov[...] = lax.dot_general(factor[...], factor[...], NT_DIMS, precision=HIGH, preferred_element_type=F32)
    oi = iota((768, 768), 0)
    order[...] = jnp.where(iota((768, 768), 1) == (oi & 15) * 48 + (oi >> 4), 1.0, 0.0).astype(BF16)

    lane_lag = iota((16, 256), 1) >> 4

    def receive(g, carry):
        batch = pl.ds(g * 16, 16)
        pltpu.make_async_copy(mrecv.at[batch], mrecv.at[batch], m_sem.at[g]).wait()
        pltpu.make_async_copy(rbuf.at[batch], rbuf.at[batch], r_sem.at[g]).wait()
        rows = dot(order[...], rbuf[batch].reshape(768, 256))
        rho = mrecv[batch, 0, :].astype(I32) & 15
        for k in range(48):
            tile = rows[k * 16 : k * 16 + 16]
            later = lane_lag < rho[:, k : k + 1]
            at = pl.ds(pl.multiple_of((k % 6) * 128 + g * 16, 16), 16)
            jw[k // 6, at, 0:256] = jnp.where(later, 0.0, tile).astype(BF16)
            jw[k // 6, at, 256:512] = jnp.where(later, tile, 0.0).astype(BF16)
        return carry

    lax.fori_loop(0, 8, receive, 0)

    first = jnp.transpose(mrecv[:, 0, :])
    second = jnp.transpose(mrecv[:, 1, :])
    code = first[0:48].astype(I32)
    key[...] = ((code & 63) >> 4) * 8 + (code >> 6)
    wgt[...] = first[64:112]
    wy[...] = second[0:48]
    pltpu.make_async_copy(sig.at[pl.ds(0, 7)], sig.at[pl.ds(0, 7)], p_sem).wait()

    rows24 = iota((24, 128), 0)

    def spread(values):
        def one(w, carry):
            cols = []
            for j in range(6):
                at = pl.ds(w * 6 + j, 1)
                cols.append(jnp.where(rows24 == key[at, :], values[at, :], 0.0))
            out = dot(split(jnp.concatenate(cols, axis=1)), jw[w])
            out = out[:24] + out[24:]
            for a in range(4):
                for h in range(2 if a < 3 else 1):
                    val = None
                    if a < 3:
                        val = out[8 * a : 8 * a + 8, h * 128 : h * 128 + 128]
                    if a > 0:
                        more = out[8 * a - 8 : 8 * a, 256 + h * 128 : 384 + h * 128]
                        val = more if val is None else val + more
                    ss[w * 7 + 2 * a + h] = val
            return carry

        lax.fori_loop(0, 8, one, 0)
        return group_transpose(ss[...]).reshape(448, 128) * sig[...].reshape(448, 128)

    def observe(g_field, phase):
        h_field = sig[...].reshape(448, 128) * jnp.dot(cov[...], g_field, precision=HIGH, preferred_element_type=F32)
        ss[...] = group_transpose(h_field.reshape(56, 8, 128))

        def one(w, carry):
            rows = []
            zero = jnp.zeros((8, 128), F32)
            for a in range(3):
                cells = [ss[w * 7 + 2 * a + h] for h in range(2)]
                for h in range(2):
                    cells.append(ss[w * 7 + 2 * a + 2 + h] if 2 * a + 2 + h < 7 else zero)
                rows.append(jnp.concatenate(cells, axis=1))
            z = lax.dot_general(split(jnp.concatenate(rows, axis=0)), jw[w], NT_DIMS, preferred_element_type=F32)
            z = z[:24] + z[24:]
            for j in range(6):
                at = pl.ds(w * 6 + j, 1)
                uval[phase, at, :] = jnp.sum(
                    jnp.where(rows24 == key[at, :], z[:, j * 128 : (j + 1) * 128], 0.0), axis=0, keepdims=True
                )
            return carry

        lax.fori_loop(0, 8, one, 0)
        ubuf[phase, m] = uval[phase]

        def send_values(d, carry):
            t = tm_at(d)
            pltpu.make_async_remote_copy(
                src_ref=uval.at[phase], dst_ref=ubuf.at[phase, m], send_sem=us_sem.at[phase], recv_sem=u_sem.at[phase],
                device_id=(r, t), device_id_type=MESH,
            ).start()
            return carry

        lax.fori_loop(1, 8, send_values, 0)
        seven = ubuf.at[phase, pl.ds(0, 7)]
        pltpu.make_async_copy(seven, seven, u_sem.at[phase]).wait()
        total = ubuf[phase, 0]
        for i in range(1, 8):
            total = total + ubuf[phase, i]
        return total

    gs[0] = spread(wy)
    u0 = observe(gs[0], 0)
    vec[0] = wgt[...] * u0
    gs[1] = spread(vec.at[0])
    v0 = observe(gs[1], 1)
    vec[1] = wgt[...] * v0

    for i, term in enumerate((wy[...] * u0, vec[0] * u0, vec[0] * v0, vec[1] * v0)):
        scal[i : i + 1, :] = jnp.sum(term, axis=0, keepdims=True)
    scal[4:8, :] = jnp.zeros((4, 128), F32)
    scal_in[r] = scal[...]

    def send_scal(i, carry):
        pltpu.make_async_remote_copy(
            src_ref=scal, dst_ref=scal_in.at[r], send_sem=cs_sem, recv_sem=c_sem,
            device_id=(region_at(i // 4, i % 4), m), device_id_type=MESH,
        ).start()
        return carry

    lax.fori_loop(1, 16, send_scal, 0)
    gs[2] = spread(vec.at[1])
    fifteen = scal_in.at[pl.ds(0, 15)]
    pltpu.make_async_copy(fifteen, fifteen, c_sem).wait()
    sums = scal_in[0]
    for i in range(1, 16):
        sums = sums + scal_in[i]
    sums = jnp.sum(sums, axis=1, keepdims=True)
    g00, g01, g11, g12 = (sums[i : i + 1, :] for i in range(4))
    a0 = g00 / (g00 + g01)
    rr1 = (1 - a0) * (1 - a0) * g00 - 2 * a0 * (1 - a0) * g01 + a0 * a0 * g11
    p, q = 1 - a0 + rr1 / g00, -a0
    a1 = rr1 / (p * p * g00 + p * (p + 2 * q) * g01 + q * (2 * p + q) * g11 + q * q * g12)
    mixed = jnp.concatenate(
        [
            (a0 + a1 * p) * gs[0] + a1 * q * gs[1],
            (1 - a0 - a1 * p) * gs[0] - (a0 + a1 * (p + q)) * gs[1] - a1 * q * gs[2],
        ],
        axis=1,
    )
    osend[...] = lax.dot_general(
        factor[...], mixed, TN_DIMS, precision=HIGH, preferred_element_type=F32
    ).reshape(8, 56, 256)

    def send_out(d, carry):
        t = tm_at(d)
        pltpu.make_async_remote_copy(
            src_ref=osend.at[t], dst_ref=obuf.at[m], send_sem=os_sem, recv_sem=o_sem,
            device_id=(r, t), device_id_type=MESH,
        ).start()
        return carry

    lax.fori_loop(1, 8, send_out, 0)
    obuf[m] = osend[m]
    seven = obuf.at[pl.ds(0, 7)]
    pltpu.make_async_copy(seven, seven, o_sem).wait()
    for k, out in ((0, x_out), (1, r_out)):
        for i in range(8):
            ptmp[:, i, :] = obuf[i, :, k * 128 : (k + 1) * 128]
        out[...] = group_transpose(ptmp[...])

    all_rows, all_meta = xs.at[pl.ds(0, 127)], mrecv.at[pl.ds(0, 127)]
    pltpu.make_async_copy(all_rows, all_rows, s_sem).wait()
    pltpu.make_async_copy(all_meta, all_meta, ms_sem).wait()
    seven = sig.at[pl.ds(0, 7)]
    pltpu.make_async_copy(seven, seven, ps_sem).wait()
    for phase in range(2):
        seven = ubuf.at[phase, pl.ds(0, 7)]
        pltpu.make_async_copy(seven, seven, us_sem.at[phase]).wait()
    pltpu.make_async_copy(fifteen, fifteen, cs_sem).wait()
    seven = obuf.at[pl.ds(0, 7)]
    pltpu.make_async_copy(seven, seven, os_sem).wait()


def local(jacobian, foot_block, foot_time, obs_weight, misfit, kept_list, kept_count, prior_std, time_factor):
    field = jax.ShapeDtypeStruct(prior_std.shape, F32)
    vmem = pl.BlockSpec(memory_space=pltpu.VMEM)
    dma = pltpu.SemaphoreType.DMA
    return pl.pallas_call(
        kernel,
        out_shape=(field, field),
        in_specs=[vmem] * 10,
        out_specs=(vmem, vmem),
        scratch_shapes=[
            pltpu.VMEM((8, 768, 256), BF16),
            pltpu.VMEM((768, 768), BF16),
            pltpu.VMEM((768, 768), BF16),
            pltpu.VMEM((128, 48, 256), BF16),
            pltpu.VMEM((128, 48, 256), BF16),
            pltpu.VMEM((16, 2, 128), F32),
            pltpu.VMEM((128, 2, 128), F32),
            pltpu.VMEM((8, 768, 512), BF16),
            pltpu.VMEM((8, 56, 128), F32),
            pltpu.VMEM((8, 56, 128), F32),
            pltpu.VMEM((448, 448), F32),
            pltpu.VMEM((48, 128), I32),
            pltpu.VMEM((48, 128), F32),
            pltpu.VMEM((48, 128), F32),
            pltpu.VMEM((2, 48, 128), F32),
            pltpu.VMEM((2, 8, 48, 128), F32),
            pltpu.VMEM((2, 48, 128), F32),
            pltpu.VMEM((56, 8, 128), F32),
            pltpu.VMEM((3, 448, 128), F32),
            pltpu.VMEM((8, 128), F32),
            pltpu.VMEM((16, 8, 128), F32),
            pltpu.VMEM((8, 56, 256), F32),
            pltpu.VMEM((8, 56, 256), F32),
            pltpu.VMEM((56, 8, 128), F32),
            dma, dma, dma((8,)), dma((8,)), dma, dma, dma((2,)), dma((2,)), dma, dma, dma, dma, dma,
        ],
        compiler_params=pltpu.CompilerParams(
            collective_id=0, has_side_effects=True, vmem_limit_bytes=48 * 2**20
        ),
    )(
        jacobian,
        foot_block.reshape(1, -1),
        foot_time.reshape(1, -1),
        foot_time.reshape(-1, 1),
        obs_weight.reshape(1, -1),
        misfit.reshape(1, -1),
        kept_list.reshape(-1, 1),
        kept_count.reshape(1, 1),
        prior_std,
        time_factor,
    )


def solution(mesh):
    rows = P(("region", "tm"))
    return jax.shard_map(
        local,
        mesh=mesh,
        in_specs=(
            P(("region", "tm"), None), rows, rows, rows, rows, rows, rows, P("tm", "region", None), P(),
        ),
        out_specs=(P("tm", "region", None), P("tm", "region", None)),
        check_vma=False,
    )
```

```python
import jax
import jax.numpy as jnp
from jax import lax
from jax.experimental import pallas as pl
from jax.experimental.pallas import tpu as pltpu
from jax.sharding import PartitionSpec as P

MESH = pl.DeviceIdType.MESH
HIGH = lax.Precision.HIGHEST
F32 = jnp.float32
BF16 = jnp.bfloat16
I32 = jnp.int32

NT_DIMS = (((1,), (1,)), ((), ()))
TN_DIMS = (((0,), (0,)), ((), ()))


def iota(shape, axis):
    return lax.broadcasted_iota(I32, shape, axis)


def dot(a, b):
    return jnp.dot(a, b, preferred_element_type=F32)


def group_transpose(x):
    shape = x.shape
    sub, grp = iota(shape, 1), iota(shape, 2) >> 4
    for s in (1, 2, 4):
        sub_bit, lane_bit = (sub & s) != 0, (grp & s) != 0
        up = pltpu.roll(pltpu.roll(x, 8 - s, 1), 16 * s, 2)
        down = pltpu.roll(pltpu.roll(x, s, 1), 128 - 16 * s, 2)
        x = jnp.where(sub_bit == lane_bit, x, jnp.where(lane_bit, up, down))
    return x


def split(x):
    low = x - x.astype(BF16).astype(F32)
    return jnp.concatenate([x, low], axis=0).astype(BF16)


def kernel(
    small, jac_in, prior_in, factor_in,
    x_out, r_out,
    jac, prior, factor, factor_t, place, order, rho_slot, picked, xs, rbuf, msend, mrecv, jw,
    psend, sig, cov, key, wgt, wy, uval, ubuf, vec,
    ss, gs, scal, scal_in, fsend, fbuf, ptmp,
    in_sem, s_sem, ms_sem, r_sem, m_sem, ps_sem, p_sem, us_sem, u_sem, cs_sem, c_sem, fs_sem, f_sem,
):
    r, m = lax.axis_index("region"), lax.axis_index("tm")
    y, x, z, c = r // 4, r % 4, m // 2, m % 2

    def region_at(dy, dx):
        return ((y + dy) % 4) * 4 + (x + dx) % 4

    def tm_at(d):
        return ((z + d // 2) % 4) * 2 + (c + d) % 2

    jac_copy = pltpu.make_async_copy(jac_in, jac, in_sem.at[0])
    prior_copy = pltpu.make_async_copy(prior_in, prior, in_sem.at[1])
    factor_copy = pltpu.make_async_copy(factor_in, factor, in_sem.at[2])
    jac_copy.start()
    prior_copy.start()
    factor_copy.start()

    barrier = pltpu.get_barrier_semaphore()

    def greet(i, carry):
        o = i // 8
        pl.semaphore_signal(
            barrier, inc=1, device_id=(region_at(o // 4, o % 4), tm_at(i % 8)), device_id_type=MESH
        )
        return carry

    lax.fori_loop(1, 128, greet, 0)

    blocks, starts = small[0:1, :].astype(I32), small[1:2, :].astype(I32)
    window = (starts * 1171) >> 16
    offset = starts - 56 * window
    named = jnp.where(iota((768, 512), 0) == small[4:5, 0:512].astype(I32), 1.0, 0.0).astype(BF16)
    kept = lax.dot_general(jnp.ones((16, 512), BF16), named, NT_DIMS, preferred_element_type=F32)[0:1]
    target = (blocks >> 3) * 8 + window
    chosen = jnp.where((iota((128, 768), 0) == target) & (kept > 0.5), 1.0, 0.0)
    before = jnp.where(iota((768, 768), 0) < iota((768, 768), 1), 1.0, 0.0).astype(BF16)
    rank = jnp.sum(chosen * dot(chosen.astype(BF16), before), axis=0, keepdims=True)
    slot = jnp.where(kept > 0.5, target * 6 + rank.astype(I32), -1)
    place[...] = jnp.where(iota((768, 768), 0) == slot, 1.0, 0.0).astype(BF16)

    row = iota((16, 768), 0)
    meta = jnp.where(row == 0, (blocks & 7).astype(F32), 0.0)
    meta = jnp.where(row == 1, offset.astype(F32), meta)
    meta = jnp.where(row == 2, small[2:3, :], meta)
    meta = jnp.where(row == 3, small[3:4, :], meta)
    meta = jnp.where(row == 4, (offset & 15).astype(F32), meta)
    meta = lax.dot_general(meta.astype(BF16), place[...], NT_DIMS, preferred_element_type=F32)
    rho_slot[...] = lax.dot_general(
        meta.astype(BF16), jnp.where(iota((16, 128), 0) == 4, 1.0, 0.0).astype(BF16), TN_DIMS,
        preferred_element_type=F32,
    ).astype(I32)
    lane = iota((1, 128), 1)
    for i in range(16):
        part = meta if i == 0 else pltpu.roll(meta, 768 - 48 * i, 1)
        part = part[:, :128]
        msend[i, 0:1, :] = jnp.where(
            lane < 64, part[0:1] * 64.0 + part[1:2], pltpu.roll(part[2:3], 64, 1)
        )
        msend[i, 1:2, :] = part[2:3] * part[3:4]

    prior_copy.wait()
    ptmp[...] = group_transpose(prior[...])
    for i in range(8):
        psend[i] = ptmp[:, i, :]
    sig[m] = psend[m]

    jac_copy.wait()
    pl.semaphore_wait(barrier, 127)
    own = m
    local_meta = pltpu.make_async_copy(msend.at[r], mrecv.at[own], m_sem.at[0])
    local_meta.start()

    lanes = iota((16, 128), 1) >> 4

    def deliver(g, carry):
        to = [region_at(g // 4 + 2 * k, g % 4 + 2 * k) for k in range(2)]
        at = [pl.multiple_of(t * 48, 16) for t in to]
        which = jnp.concatenate([place[pl.ds(a, 48), :] for a in at], axis=0)
        for l in range(0, 2048, 256):
            picked[:, l : l + 256] = dot(which, jac[:, l : l + 256])
        for k in range(2):

            def turn(i, carry, k=k):
                rows = pl.ds(pl.multiple_of(k * 48 + i * 16, 16), 16)
                out = pl.ds(pl.multiple_of(i * 16, 16), 16)
                rho = rho_slot[pl.ds(pl.multiple_of(at[k] + i * 16, 16), 16), :]
                parts = [picked[rows, l * 128 : (l + 1) * 128] for l in range(16)]
                for s in (1, 2, 4, 8):
                    bit = (rho & s) != 0
                    parts = [jnp.where(bit, parts[(l - s) % 16], parts[l]) for l in range(16)]
                for half in range(2):
                    v = parts[half * 8 : half * 8 + 8]
                    for s in (1, 2, 4):
                        bit = (lanes & s) != 0
                        new = list(v)
                        for n in range(8):
                            if n & s == 0:
                                new[n] = jnp.where(bit, pltpu.roll(v[n + s], 16 * s, 1), v[n])
                                new[n + s] = jnp.where(bit, v[n + s], pltpu.roll(v[n], 128 - 16 * s, 1))
                        v = new
                    for n in range(8):
                        xs[g * 16 + k * 8 + n, out, half * 128 : (half + 1) * 128] = v[n].astype(BF16)
                return carry

            lax.fori_loop(0, 3, turn, 0)

        def send(k, d):
            t = tm_at(d)
            here = g * 16 + k * 8 + m
            pltpu.make_async_remote_copy(
                src_ref=msend.at[to[k]], dst_ref=mrecv.at[here], send_sem=ms_sem, recv_sem=m_sem.at[g],
                device_id=(to[k], t), device_id_type=MESH,
            ).start()
            pltpu.make_async_remote_copy(
                src_ref=xs.at[g * 16 + k * 8 + t], dst_ref=rbuf.at[here], send_sem=s_sem, recv_sem=r_sem.at[g],
                device_id=(to[k], t), device_id_type=MESH,
            ).start()

        def send_two(d, carry):
            send(0, d)
            send(1, d)
            return carry

        @pl.when(g > 0)
        def _():
            send(0, 0)

        send(1, 0)
        lax.fori_loop(1, 8, send_two, 0)
        return carry

    lax.fori_loop(0, 8, deliver, 0)
    local_rows = pltpu.make_async_copy(xs.at[own], rbuf.at[own], r_sem.at[0])
    local_rows.start()

    def send_prior(d, carry):
        t = tm_at(d)
        pltpu.make_async_remote_copy(
            src_ref=psend.at[t], dst_ref=sig.at[m], send_sem=ps_sem, recv_sem=p_sem,
            device_id=(r, t), device_id_type=MESH,
        ).start()
        return carry

    lax.fori_loop(1, 8, send_prior, 0)

    factor_copy.wait()
    cov[...] = lax.dot_general(factor[...], factor[...], NT_DIMS, precision=HIGH, preferred_element_type=F32)
    factor_t[...] = jnp.transpose(factor[...])
    oi = iota((768, 768), 0)
    order[...] = jnp.where(iota((768, 768), 1) == (oi & 15) * 48 + (oi >> 4), 1.0, 0.0).astype(BF16)

    lane_lag = iota((16, 256), 1) >> 4

    def receive(g, carry):
        batch = pl.ds(g * 16, 16)
        pltpu.make_async_copy(mrecv.at[batch], mrecv.at[batch], m_sem.at[g]).wait()
        pltpu.make_async_copy(rbuf.at[batch], rbuf.at[batch], r_sem.at[g]).wait()
        rows = dot(order[...], rbuf[batch].reshape(768, 256))
        rho = mrecv[batch, 0, :].astype(I32) & 15
        for k in range(48):
            tile = rows[k * 16 : k * 16 + 16]
            later = lane_lag < rho[:, k : k + 1]
            at = pl.ds(pl.multiple_of((k % 6) * 128 + g * 16, 16), 16)
            jw[k // 6, at, 0:256] = jnp.where(later, 0.0, tile).astype(BF16)
            jw[k // 6, at, 256:512] = jnp.where(later, tile, 0.0).astype(BF16)
        return carry

    lax.fori_loop(0, 8, receive, 0)

    first = jnp.transpose(mrecv[:, 0, :])
    second = jnp.transpose(mrecv[:, 1, :])
    code = first[0:48].astype(I32)
    key[...] = ((code & 63) >> 4) * 8 + (code >> 6)
    wgt[...] = first[64:112]
    wy[...] = second[0:48]
    pltpu.make_async_copy(sig.at[pl.ds(0, 7)], sig.at[pl.ds(0, 7)], p_sem).wait()

    rows24 = iota((24, 128), 0)

    def spread(values, ready):
        def one(w, carry):
            cols = []
            for j in range(6):
                at = pl.ds(w * 6 + j, 1)
                cols.append(jnp.where(rows24 == key[at, :], values[at, :], 0.0))
            out = dot(split(jnp.concatenate(cols, axis=1)), jw[w])
            out = out[:24] + out[24:]
            for a in range(4):
                for h in range(2 if a < 3 else 1):
                    val = None
                    if a < 3:
                        val = out[8 * a : 8 * a + 8, h * 128 : h * 128 + 128]
                    if a > 0:
                        more = out[8 * a - 8 : 8 * a, 256 + h * 128 : 384 + h * 128]
                        val = more if val is None else val + more
                    ss[w * 7 + 2 * a + h] = val
            return carry

        for half in range(2):
            ready(half)
            lax.fori_loop(half * 4, half * 4 + 4, one, 0)
        return group_transpose(ss[...]).reshape(448, 128) * sig[...].reshape(448, 128)

    def observe(g_field, phase):
        h_field = sig[...].reshape(448, 128) * jnp.dot(cov[...], g_field, precision=HIGH, preferred_element_type=F32)
        ss[...] = group_transpose(h_field.reshape(56, 8, 128))

        def one(w, carry):
            rows = []
            zero = jnp.zeros((8, 128), F32)
            for a in range(3):
                cells = [ss[w * 7 + 2 * a + h] for h in range(2)]
                for h in range(2):
                    cells.append(ss[w * 7 + 2 * a + 2 + h] if 2 * a + 2 + h < 7 else zero)
                rows.append(jnp.concatenate(cells, axis=1))
            v = lax.dot_general(split(jnp.concatenate(rows, axis=0)), jw[w], NT_DIMS, preferred_element_type=F32)
            v = v[:24] + v[24:]
            for j in range(6):
                uval[phase, pl.ds(w * 6 + j, 1), :] = jnp.sum(
                    jnp.where(rows24 == key[pl.ds(w * 6 + j, 1), :], v[:, j * 128 : (j + 1) * 128], 0.0),
                    axis=0, keepdims=True,
                )
            return carry

        for half in range(2):
            lax.fori_loop(half * 4, half * 4 + 4, one, 0)
            mine = uval.at[phase, pl.ds(half * 24, 24)]

            def send_values(d, carry, half=half, mine=mine):
                t = tm_at(d)
                pltpu.make_async_remote_copy(
                    src_ref=mine, dst_ref=ubuf.at[phase, half, m],
                    send_sem=us_sem.at[phase, half], recv_sem=u_sem.at[phase, half],
                    device_id=(r, t), device_id_type=MESH,
                ).start()
                return carry

            lax.fori_loop(1, 8, send_values, 0)
            ubuf[phase, half, m] = uval[phase, half * 24 : half * 24 + 24, :]

    def collect(phase):
        def ready(half):
            seven = ubuf.at[phase, half, pl.ds(0, 7)]
            pltpu.make_async_copy(seven, seven, u_sem.at[phase, half]).wait()
            total = ubuf[phase, half, 0]
            for i in range(1, 8):
                total = total + ubuf[phase, half, i]
            rows = slice(half * 24, half * 24 + 24)
            weighted = wgt[rows, :] * total
            vec[phase, rows, :] = weighted
            if phase == 0:
                terms = (wy[rows, :] * total, weighted * total)
            else:
                terms = (vec[0, rows, :] * total, weighted * total)
            for i, term in enumerate(terms):
                term = jnp.sum(term, axis=0, keepdims=True)
                at = slice(2 * phase + i, 2 * phase + i + 1)
                scal[at, :] = term if half == 0 else scal[at, :] + term

        return ready

    def send_field(k):
        fsend[k] = jnp.dot(
            factor_t[...], gs[k], precision=HIGH, preferred_element_type=F32
        ).reshape(8, 56, 128)

        def send(d, carry):
            t = tm_at(d)
            pltpu.make_async_remote_copy(
                src_ref=fsend.at[k, t], dst_ref=fbuf.at[k, m], send_sem=fs_sem.at[k], recv_sem=f_sem.at[k],
                device_id=(r, t), device_id_type=MESH,
            ).start()
            return carry

        lax.fori_loop(1, 8, send, 0)
        fbuf[k, m] = fsend[k, m]

    def wait_field(k):
        seven = fbuf.at[k, pl.ds(0, 7)]
        pltpu.make_async_copy(seven, seven, f_sem.at[k]).wait()

    scal[4:8, :] = jnp.zeros((4, 128), F32)
    gs[0] = spread(wy, lambda half: None)
    observe(gs[0], 0)
    send_field(0)
    gs[1] = spread(vec.at[0], collect(0))
    observe(gs[1], 1)
    send_field(1)
    gs[2] = spread(vec.at[1], collect(1))
    send_field(2)

    scal_in[r] = scal[...]

    def send_scal(i, carry):
        pltpu.make_async_remote_copy(
            src_ref=scal, dst_ref=scal_in.at[r], send_sem=cs_sem, recv_sem=c_sem,
            device_id=(region_at(i // 4, i % 4), m), device_id_type=MESH,
        ).start()
        return carry

    lax.fori_loop(1, 16, send_scal, 0)
    fifteen = scal_in.at[pl.ds(0, 15)]
    pltpu.make_async_copy(fifteen, fifteen, c_sem).wait()
    sums = scal_in[0]
    for i in range(1, 16):
        sums = sums + scal_in[i]
    sums = jnp.sum(sums, axis=1, keepdims=True)
    g00, g01, g11, g12 = (sums[i : i + 1, :] for i in range(4))
    a0 = g00 / (g00 + g01)
    rr1 = (1 - a0) * (1 - a0) * g00 - 2 * a0 * (1 - a0) * g01 + a0 * a0 * g11
    p, q = 1 - a0 + rr1 / g00, -a0
    a1 = rr1 / (p * p * g00 + p * (p + 2 * q) * g01 + q * (2 * p + q) * g11 + q * q * g12)
    wait_field(0)
    wait_field(1)
    for i in range(8):
        ptmp[:, i, :] = (a0 + a1 * p) * fbuf[0, i] + a1 * q * fbuf[1, i]
    x_out[...] = group_transpose(ptmp[...])
    for i in range(8):
        fbuf[0, i] = (1 - a0 - a1 * p) * fbuf[0, i] - (a0 + a1 * (p + q)) * fbuf[1, i]
    wait_field(2)
    for i in range(8):
        ptmp[:, i, :] = fbuf[0, i] - a1 * q * fbuf[2, i]
    r_out[...] = group_transpose(ptmp[...])

    all_rows, all_meta = xs.at[pl.ds(0, 127)], mrecv.at[pl.ds(0, 127)]
    pltpu.make_async_copy(all_rows, all_rows, s_sem).wait()
    pltpu.make_async_copy(all_meta, all_meta, ms_sem).wait()
    seven = sig.at[pl.ds(0, 7)]
    pltpu.make_async_copy(seven, seven, ps_sem).wait()
    for phase in range(2):
        for half in range(2):
            seven = ubuf.at[phase, half, pl.ds(0, 7)]
            pltpu.make_async_copy(seven, seven, us_sem.at[phase, half]).wait()
    pltpu.make_async_copy(fifteen, fifteen, cs_sem).wait()
    for k in range(3):
        seven = fbuf.at[k, pl.ds(0, 7)]
        pltpu.make_async_copy(seven, seven, fs_sem.at[k]).wait()


def local(jacobian, foot_block, foot_time, obs_weight, misfit, kept_list, kept_count, prior_std, time_factor):
    field = jax.ShapeDtypeStruct(prior_std.shape, F32)
    vmem = pl.BlockSpec(memory_space=pltpu.VMEM)
    anywhere = pl.BlockSpec(memory_space=pl.ANY)
    dma = pltpu.SemaphoreType.DMA
    pool, keep = foot_block.shape[0], kept_list.shape[0]
    named = jnp.where(jnp.arange(keep, dtype=I32) < kept_count[0], kept_list, -1)
    named = jnp.pad(named, (0, pool - keep), constant_values=-1)
    row = lax.broadcasted_iota(I32, (8, pool), 0)
    small = jnp.zeros((8, pool), F32)
    for i, values in enumerate((foot_block, foot_time, obs_weight, misfit, named)):
        small = jnp.where(row == i, values.astype(F32)[None, :], small)
    return pl.pallas_call(
        kernel,
        out_shape=(field, field),
        in_specs=[vmem] + [anywhere] * 3,
        out_specs=(vmem, vmem),
        scratch_shapes=[
            pltpu.VMEM((768, 2048), BF16),
            pltpu.VMEM((56, 8, 128), F32),
            pltpu.VMEM((448, 448), F32),
            pltpu.VMEM((448, 448), F32),
            pltpu.VMEM((768, 768), BF16),
            pltpu.VMEM((768, 768), BF16),
            pltpu.VMEM((768, 128), I32),
            pltpu.VMEM((96, 2048), F32),
            pltpu.VMEM((128, 48, 256), BF16),
            pltpu.VMEM((128, 48, 256), BF16),
            pltpu.VMEM((16, 2, 128), F32),
            pltpu.VMEM((128, 2, 128), F32),
            pltpu.VMEM((8, 768, 512), BF16),
            pltpu.VMEM((8, 56, 128), F32),
            pltpu.VMEM((8, 56, 128), F32),
            pltpu.VMEM((448, 448), F32),
            pltpu.VMEM((48, 128), I32),
            pltpu.VMEM((48, 128), F32),
            pltpu.VMEM((48, 128), F32),
            pltpu.VMEM((2, 48, 128), F32),
            pltpu.VMEM((2, 2, 8, 24, 128), F32),
            pltpu.VMEM((2, 48, 128), F32),
            pltpu.VMEM((56, 8, 128), F32),
            pltpu.VMEM((3, 448, 128), F32),
            pltpu.VMEM((8, 128), F32),
            pltpu.VMEM((16, 8, 128), F32),
            pltpu.VMEM((3, 8, 56, 128), F32),
            pltpu.VMEM((3, 8, 56, 128), F32),
            pltpu.VMEM((56, 8, 128), F32),
            dma((3,)), dma, dma, dma((8,)), dma((8,)), dma, dma, dma((2, 2)), dma((2, 2)), dma, dma, dma((3,)), dma((3,)),
        ],
        compiler_params=pltpu.CompilerParams(
            collective_id=0, has_side_effects=True, vmem_limit_bytes=48 * 2**20
        ),
    )(small, jacobian, prior_std, time_factor)


def solution(mesh):
    rows = P(("region", "tm"))
    return jax.shard_map(
        local,
        mesh=mesh,
        in_specs=(
            P(("region", "tm"), None), rows, rows, rows, rows, rows, rows, P("tm", "region", None), P(),
        ),
        out_specs=(P("tm", "region", None), P("tm", "region", None)),
        check_vma=False,
    )
```

```python
import jax
import jax.numpy as jnp
from jax import lax
from jax.experimental import pallas as pl
from jax.experimental.pallas import tpu as pltpu
from jax.sharding import PartitionSpec as P

MESH = pl.DeviceIdType.MESH
HIGH = lax.Precision.HIGHEST
F32 = jnp.float32
BF16 = jnp.bfloat16
I32 = jnp.int32

NT_DIMS = (((1,), (1,)), ((), ()))
TN_DIMS = (((0,), (0,)), ((), ()))


def iota(shape, axis):
    return lax.broadcasted_iota(I32, shape, axis)


def dot(a, b):
    return jnp.dot(a, b, preferred_element_type=F32)


def group_transpose(x):
    shape = x.shape
    sub, grp = iota(shape, 1), iota(shape, 2) >> 4
    for s in (1, 2, 4):
        sub_bit, lane_bit = (sub & s) != 0, (grp & s) != 0
        up = pltpu.roll(pltpu.roll(x, 8 - s, 1), 16 * s, 2)
        down = pltpu.roll(pltpu.roll(x, s, 1), 128 - 16 * s, 2)
        x = jnp.where(sub_bit == lane_bit, x, jnp.where(lane_bit, up, down))
    return x


def split(x):
    low = x - x.astype(BF16).astype(F32)
    return jnp.concatenate([x, low], axis=0).astype(BF16)


def in_time(pair, x):
    n = x.shape[0]
    high = x.astype(BF16)
    low = (x - high.astype(F32)).astype(BF16)
    out = dot(pair[0:n, :], jnp.concatenate([high, low], axis=1))
    return out[:, 0:128] + out[:, 128:256] + dot(pair[n : 2 * n, :], high)


def kernel(
    fb_in, ft_in, w_in, y_in, list_in, count_in, jac_in, prior_in, factor_in,
    x_out, r_out,
    jac, prior, factor, factor_t, place, order, rho_slot, picked, xs, rbuf, msend, mrecv, jw,
    psend, sig, cov, key, wgt, wy, uval, ubuf, vec,
    ss, gs, scal, scal_in, fsend, fbuf, ptmp,
    entered, in_sem, s_sem, ms_sem, r_sem, m_sem, ps_sem, p_sem, us_sem, u_sem, cs_sem, c_sem, fs_sem, f_sem,
):
    r, m = lax.axis_index("region"), lax.axis_index("tm")
    y, x, z, c = r // 4, r % 4, m // 2, m % 2

    def region_at(dy, dx):
        return ((y + dy) % 4) * 4 + (x + dx) % 4

    def tm_at(d):
        return ((z + d // 2) % 4) * 2 + (c + d) % 2

    jac_copy = pltpu.make_async_copy(jac_in, jac, in_sem.at[0])
    prior_copy = pltpu.make_async_copy(prior_in, prior, in_sem.at[1])
    factor_copy = pltpu.make_async_copy(factor_in, factor, in_sem.at[2])
    jac_copy.start()
    prior_copy.start()
    factor_copy.start()

    barrier = pltpu.get_barrier_semaphore()

    def greet_group(d, carry):
        pl.semaphore_signal(barrier, inc=1, device_id=(r, tm_at(d)), device_id_type=MESH)
        return carry

    def greet_region(i, carry):
        pl.semaphore_signal(barrier, inc=1, device_id=(region_at(i // 4, i % 4), m), device_id_type=MESH)
        return carry

    lax.fori_loop(1, 16, greet_region, 0)
    lax.fori_loop(1, 8, greet_group, 0)

    def as_row(ref):
        return ref[...].reshape(1, -1)

    blocks, starts = as_row(fb_in), as_row(ft_in)
    window = (starts * 1171) >> 16
    offset = starts - 56 * window
    named = jnp.where(iota((1, 512), 1) < count_in[0], as_row(list_in), -1)
    named = jnp.where(iota((768, 512), 0) == named, 1.0, 0.0).astype(BF16)
    kept = lax.dot_general(jnp.ones((16, 512), BF16), named, NT_DIMS, preferred_element_type=F32)[0:1]
    target = (blocks >> 3) * 8 + window
    chosen = jnp.where((iota((128, 768), 0) == target) & (kept > 0.5), 1.0, 0.0)
    before = jnp.where(iota((768, 768), 0) < iota((768, 768), 1), 1.0, 0.0).astype(BF16)
    rank = jnp.sum(chosen * dot(chosen.astype(BF16), before), axis=0, keepdims=True)
    slot = jnp.where(kept > 0.5, target * 6 + rank.astype(I32), -1)
    place[...] = jnp.where(iota((768, 768), 0) == slot, 1.0, 0.0).astype(BF16)

    row = iota((16, 768), 0)
    meta = jnp.where(row == 0, (blocks & 7).astype(F32), 0.0)
    meta = jnp.where(row == 1, offset.astype(F32), meta)
    meta = jnp.where(row == 2, as_row(w_in).astype(F32), meta)
    meta = jnp.where(row == 3, as_row(y_in).astype(F32), meta)
    meta = jnp.where(row == 4, (offset & 15).astype(F32), meta)
    meta = lax.dot_general(meta.astype(BF16), place[...], NT_DIMS, preferred_element_type=F32)
    rho_slot[...] = lax.dot_general(
        meta.astype(BF16), jnp.where(iota((16, 128), 0) == 4, 1.0, 0.0).astype(BF16), TN_DIMS,
        preferred_element_type=F32,
    ).astype(I32)
    lane = iota((1, 128), 1)
    for i in range(16):
        part = meta if i == 0 else pltpu.roll(meta, 768 - 48 * i, 1)
        part = part[:, :128]
        msend[i, 0:1, :] = jnp.where(
            lane < 64, part[0:1] * 64.0 + part[1:2], pltpu.roll(part[2:3], 64, 1)
        )
        msend[i, 1:2, :] = part[2:3] * part[3:4]

    pl.semaphore_wait(barrier, 22)

    def vouch(d, carry):
        pl.semaphore_signal(entered, inc=1, device_id=(r, tm_at(d)), device_id_type=MESH)
        return carry

    lax.fori_loop(1, 8, vouch, 0)

    prior_copy.wait()
    ptmp[...] = group_transpose(prior[...])
    for i in range(8):
        psend[i] = ptmp[:, i, :]
    sig[m] = psend[m]

    jac_copy.wait()
    pl.semaphore_wait(entered, 7)
    own = m
    local_meta = pltpu.make_async_copy(msend.at[r], mrecv.at[own], m_sem.at[0])
    local_meta.start()

    lanes = iota((16, 128), 1) >> 4

    def deliver(g, carry):
        to = [region_at(g // 4 + 2 * k, g % 4 + 2 * k) for k in range(2)]
        at = [pl.multiple_of(t * 48, 16) for t in to]
        which = jnp.concatenate([place[pl.ds(a, 48), :] for a in at], axis=0)
        for l in range(0, 2048, 256):
            picked[:, l : l + 256] = dot(which, jac[:, l : l + 256])
        for k in range(2):

            def turn(i, carry, k=k):
                rows = pl.ds(pl.multiple_of(k * 48 + i * 16, 16), 16)
                out = pl.ds(pl.multiple_of(i * 16, 16), 16)
                rho = rho_slot[pl.ds(pl.multiple_of(at[k] + i * 16, 16), 16), :]
                parts = [picked[rows, l * 128 : (l + 1) * 128] for l in range(16)]
                for s in (1, 2, 4, 8):
                    bit = (rho & s) != 0
                    parts = [jnp.where(bit, parts[(l - s) % 16], parts[l]) for l in range(16)]
                for half in range(2):
                    v = parts[half * 8 : half * 8 + 8]
                    for s in (1, 2, 4):
                        bit = (lanes & s) != 0
                        new = list(v)
                        for n in range(8):
                            if n & s == 0:
                                new[n] = jnp.where(bit, pltpu.roll(v[n + s], 16 * s, 1), v[n])
                                new[n + s] = jnp.where(bit, v[n + s], pltpu.roll(v[n], 128 - 16 * s, 1))
                        v = new
                    for n in range(8):
                        xs[g * 16 + k * 8 + n, out, half * 128 : (half + 1) * 128] = v[n].astype(BF16)
                return carry

            lax.fori_loop(0, 3, turn, 0)

        def send(k, d):
            t = tm_at(d)
            here = g * 16 + k * 8 + m
            pltpu.make_async_remote_copy(
                src_ref=msend.at[to[k]], dst_ref=mrecv.at[here], send_sem=ms_sem, recv_sem=m_sem.at[g],
                device_id=(to[k], t), device_id_type=MESH,
            ).start()
            pltpu.make_async_remote_copy(
                src_ref=xs.at[g * 16 + k * 8 + t], dst_ref=rbuf.at[here], send_sem=s_sem, recv_sem=r_sem.at[g],
                device_id=(to[k], t), device_id_type=MESH,
            ).start()

        def send_two(d, carry):
            send(0, d)
            send(1, d)
            return carry

        @pl.when(g > 0)
        def _():
            send(0, 0)

        send(1, 0)
        lax.fori_loop(1, 8, send_two, 0)
        return carry

    lax.fori_loop(0, 8, deliver, 0)
    local_rows = pltpu.make_async_copy(xs.at[own], rbuf.at[own], r_sem.at[0])
    local_rows.start()

    def send_prior(d, carry):
        t = tm_at(d)
        pltpu.make_async_remote_copy(
            src_ref=psend.at[t], dst_ref=sig.at[m], send_sem=ps_sem, recv_sem=p_sem,
            device_id=(r, t), device_id_type=MESH,
        ).start()
        return carry

    lax.fori_loop(1, 8, send_prior, 0)

    factor_copy.wait()
    product = lax.dot_general(factor[...], factor[...], NT_DIMS, precision=HIGH, preferred_element_type=F32)
    for ref, value in ((cov, product), (factor_t, jnp.transpose(factor[...]))):
        ref[0:448, :] = value.astype(BF16)
        ref[448:896, :] = (value - value.astype(BF16).astype(F32)).astype(BF16)
    oi = iota((768, 768), 0)
    order[...] = jnp.where(iota((768, 768), 1) == (oi & 15) * 48 + (oi >> 4), 1.0, 0.0).astype(BF16)

    lane_lag = iota((16, 256), 1) >> 4

    def receive(g, carry):
        batch = pl.ds(g * 16, 16)
        pltpu.make_async_copy(mrecv.at[batch], mrecv.at[batch], m_sem.at[g]).wait()
        pltpu.make_async_copy(rbuf.at[batch], rbuf.at[batch], r_sem.at[g]).wait()
        rows = dot(order[...], rbuf[batch].reshape(768, 256))
        rho = mrecv[batch, 0, :].astype(I32) & 15
        for k in range(48):
            tile = rows[k * 16 : k * 16 + 16]
            later = lane_lag < rho[:, k : k + 1]
            at = pl.ds(pl.multiple_of((k % 6) * 128 + g * 16, 16), 16)
            jw[k // 6, at, 0:256] = jnp.where(later, 0.0, tile).astype(BF16)
            jw[k // 6, at, 256:512] = jnp.where(later, tile, 0.0).astype(BF16)
        return carry

    lax.fori_loop(0, 8, receive, 0)

    first = jnp.transpose(mrecv[:, 0, :])
    second = jnp.transpose(mrecv[:, 1, :])
    code = first[0:48].astype(I32)
    key[...] = ((code & 63) >> 4) * 8 + (code >> 6)
    wgt[...] = first[64:112]
    wy[...] = second[0:48]
    pltpu.make_async_copy(sig.at[pl.ds(0, 7)], sig.at[pl.ds(0, 7)], p_sem).wait()

    rows24 = iota((24, 128), 0)

    def spread(values, ready):
        def one(w, carry):
            cols = []
            for j in range(6):
                at = pl.ds(w * 6 + j, 1)
                cols.append(jnp.where(rows24 == key[at, :], values[at, :], 0.0))
            out = dot(split(jnp.concatenate(cols, axis=1)), jw[w])
            out = out[:24] + out[24:]
            for a in range(4):
                for h in range(2 if a < 3 else 1):
                    val = None
                    if a < 3:
                        val = out[8 * a : 8 * a + 8, h * 128 : h * 128 + 128]
                    if a > 0:
                        more = out[8 * a - 8 : 8 * a, 256 + h * 128 : 384 + h * 128]
                        val = more if val is None else val + more
                    ss[w * 7 + 2 * a + h] = val
            return carry

        for half in range(2):
            ready(half)
            [one(w, 0) for w in range(half * 4, half * 4 + 4)]
        return group_transpose(ss[...]).reshape(448, 128) * sig[...].reshape(448, 128)

    def observe(g_field, phase):
        h_field = sig[...].reshape(448, 128) * in_time(cov, g_field)
        ss[...] = group_transpose(h_field.reshape(56, 8, 128))

        def one(w, carry):
            rows = []
            zero = jnp.zeros((8, 128), F32)
            for a in range(3):
                cells = [ss[w * 7 + 2 * a + h] for h in range(2)]
                for h in range(2):
                    cells.append(ss[w * 7 + 2 * a + 2 + h] if 2 * a + 2 + h < 7 else zero)
                rows.append(jnp.concatenate(cells, axis=1))
            v = lax.dot_general(split(jnp.concatenate(rows, axis=0)), jw[w], NT_DIMS, preferred_element_type=F32)
            v = v[:24] + v[24:]
            for j in range(6):
                uval[phase, pl.ds(w * 6 + j, 1), :] = jnp.sum(
                    jnp.where(rows24 == key[pl.ds(w * 6 + j, 1), :], v[:, j * 128 : (j + 1) * 128], 0.0),
                    axis=0, keepdims=True,
                )
            return carry

        for half in range(2):
            [one(w, 0) for w in range(half * 4, half * 4 + 4)]
            mine = uval.at[phase, pl.ds(half * 24, 24)]

            def send_values(d, carry, half=half, mine=mine):
                t = tm_at(d)
                pltpu.make_async_remote_copy(
                    src_ref=mine, dst_ref=ubuf.at[phase, half, m],
                    send_sem=us_sem.at[phase, half], recv_sem=u_sem.at[phase, half],
                    device_id=(r, t), device_id_type=MESH,
                ).start()
                return carry

            lax.fori_loop(1, 8, send_values, 0)
            ubuf[phase, half, m] = uval[phase, half * 24 : half * 24 + 24, :]

    def collect(phase):
        def ready(half):
            seven = ubuf.at[phase, half, pl.ds(0, 7)]
            pltpu.make_async_copy(seven, seven, u_sem.at[phase, half]).wait()
            total = ubuf[phase, half, 0]
            for i in range(1, 8):
                total = total + ubuf[phase, half, i]
            rows = slice(half * 24, half * 24 + 24)
            weighted = wgt[rows, :] * total
            vec[phase, rows, :] = weighted
            if phase == 0:
                terms = (wy[rows, :] * total, weighted * total)
            else:
                terms = (vec[0, rows, :] * total, weighted * total)
            for i, term in enumerate(terms):
                term = jnp.sum(term, axis=0, keepdims=True)
                at = slice(2 * phase + i, 2 * phase + i + 1)
                scal[at, :] = term if half == 0 else scal[at, :] + term

        return ready

    def send_field(k):
        fsend[k] = in_time(factor_t, gs[k]).reshape(8, 56, 128)

        def send(d, carry):
            t = tm_at(d)
            pltpu.make_async_remote_copy(
                src_ref=fsend.at[k, t], dst_ref=fbuf.at[k, m], send_sem=fs_sem.at[k], recv_sem=f_sem.at[k],
                device_id=(r, t), device_id_type=MESH,
            ).start()
            return carry

        lax.fori_loop(1, 8, send, 0)
        fbuf[k, m] = fsend[k, m]

    def wait_field(k):
        seven = fbuf.at[k, pl.ds(0, 7)]
        pltpu.make_async_copy(seven, seven, f_sem.at[k]).wait()

    scal[4:8, :] = jnp.zeros((4, 128), F32)
    gs[0] = spread(wy, lambda half: None)
    observe(gs[0], 0)
    send_field(0)
    gs[1] = spread(vec.at[0], collect(0))
    observe(gs[1], 1)
    send_field(1)
    gs[2] = spread(vec.at[1], collect(1))
    send_field(2)

    scal_in[r] = scal[...]

    def send_scal(i, carry):
        pltpu.make_async_remote_copy(
            src_ref=scal, dst_ref=scal_in.at[r], send_sem=cs_sem, recv_sem=c_sem,
            device_id=(region_at(i // 4, i % 4), m), device_id_type=MESH,
        ).start()
        return carry

    lax.fori_loop(1, 16, send_scal, 0)
    fifteen = scal_in.at[pl.ds(0, 15)]
    pltpu.make_async_copy(fifteen, fifteen, c_sem).wait()
    sums = scal_in[0]
    for i in range(1, 16):
        sums = sums + scal_in[i]
    sums = jnp.sum(sums, axis=1, keepdims=True)
    g00, g01, g11, g12 = (sums[i : i + 1, :] for i in range(4))
    a0 = g00 / (g00 + g01)
    rr1 = (1 - a0) * (1 - a0) * g00 - 2 * a0 * (1 - a0) * g01 + a0 * a0 * g11
    p, q = 1 - a0 + rr1 / g00, -a0
    a1 = rr1 / (p * p * g00 + p * (p + 2 * q) * g01 + q * (2 * p + q) * g11 + q * q * g12)
    wait_field(0)
    wait_field(1)
    for i in range(8):
        ptmp[:, i, :] = (a0 + a1 * p) * fbuf[0, i] + a1 * q * fbuf[1, i]
    x_out[...] = group_transpose(ptmp[...])
    for i in range(8):
        fbuf[0, i] = (1 - a0 - a1 * p) * fbuf[0, i] - (a0 + a1 * (p + q)) * fbuf[1, i]
    wait_field(2)
    for i in range(8):
        ptmp[:, i, :] = fbuf[0, i] - a1 * q * fbuf[2, i]
    r_out[...] = group_transpose(ptmp[...])

    all_rows, all_meta = xs.at[pl.ds(0, 127)], mrecv.at[pl.ds(0, 127)]
    pltpu.make_async_copy(all_rows, all_rows, s_sem).wait()
    pltpu.make_async_copy(all_meta, all_meta, ms_sem).wait()
    seven = sig.at[pl.ds(0, 7)]
    pltpu.make_async_copy(seven, seven, ps_sem).wait()
    for phase in range(2):
        for half in range(2):
            seven = ubuf.at[phase, half, pl.ds(0, 7)]
            pltpu.make_async_copy(seven, seven, us_sem.at[phase, half]).wait()
    pltpu.make_async_copy(fifteen, fifteen, cs_sem).wait()
    for k in range(3):
        seven = fbuf.at[k, pl.ds(0, 7)]
        pltpu.make_async_copy(seven, seven, fs_sem.at[k]).wait()


def local(jacobian, foot_block, foot_time, obs_weight, misfit, kept_list, kept_count, prior_std, time_factor):
    field = jax.ShapeDtypeStruct(prior_std.shape, F32)
    vmem = pl.BlockSpec(memory_space=pltpu.VMEM)
    hbm = pl.BlockSpec(memory_space=pltpu.HBM)
    dma = pltpu.SemaphoreType.DMA
    return pl.pallas_call(
        kernel,
        out_shape=(field, field),
        in_specs=[vmem] * 5 + [pl.BlockSpec(memory_space=pltpu.SMEM)] + [hbm] * 3,
        out_specs=(vmem, vmem),
        scratch_shapes=[
            pltpu.VMEM((768, 2048), BF16),
            pltpu.VMEM((56, 8, 128), F32),
            pltpu.VMEM((448, 448), F32),
            pltpu.VMEM((896, 448), BF16),
            pltpu.VMEM((768, 768), BF16),
            pltpu.VMEM((768, 768), BF16),
            pltpu.VMEM((768, 128), I32),
            pltpu.VMEM((96, 2048), F32),
            pltpu.VMEM((128, 48, 256), BF16),
            pltpu.VMEM((128, 48, 256), BF16),
            pltpu.VMEM((16, 2, 128), F32),
            pltpu.VMEM((128, 2, 128), F32),
            pltpu.VMEM((8, 768, 512), BF16),
            pltpu.VMEM((8, 56, 128), F32),
            pltpu.VMEM((8, 56, 128), F32),
            pltpu.VMEM((896, 448), BF16),
            pltpu.VMEM((48, 128), I32),
            pltpu.VMEM((48, 128), F32),
            pltpu.VMEM((48, 128), F32),
            pltpu.VMEM((2, 48, 128), F32),
            pltpu.VMEM((2, 2, 8, 24, 128), F32),
            pltpu.VMEM((2, 48, 128), F32),
            pltpu.VMEM((56, 8, 128), F32),
            pltpu.VMEM((3, 448, 128), F32),
            pltpu.VMEM((8, 128), F32),
            pltpu.VMEM((16, 8, 128), F32),
            pltpu.VMEM((3, 8, 56, 128), F32),
            pltpu.VMEM((3, 8, 56, 128), F32),
            pltpu.VMEM((56, 8, 128), F32),
            pltpu.SemaphoreType.REGULAR, dma((3,)), dma, dma, dma((8,)), dma((8,)), dma, dma, dma((2, 2)), dma((2, 2)), dma, dma, dma((3,)), dma((3,)),
        ],
        compiler_params=pltpu.CompilerParams(
            collective_id=0, has_side_effects=True, vmem_limit_bytes=60 * 2**20
        ),
    )(foot_block, foot_time, obs_weight, misfit, kept_list, kept_count, jacobian, prior_std, time_factor)


def solution(mesh):
    rows = P(("region", "tm"))
    return jax.shard_map(
        local,
        mesh=mesh,
        in_specs=(
            P(("region", "tm"), None), rows, rows, rows, rows, rows, rows, P("tm", "region", None), P(),
        ),
        out_specs=(P("tm", "region", None), P("tm", "region", None)),
        check_vma=False,
    )
```

```python
import jax
import jax.numpy as jnp
from jax import lax
from jax.experimental import pallas as pl
from jax.experimental.pallas import tpu as pltpu
from jax.sharding import PartitionSpec as P

MESH = pl.DeviceIdType.MESH
HIGH = lax.Precision.HIGHEST
F32 = jnp.float32
BF16 = jnp.bfloat16
I32 = jnp.int32

NT_DIMS = (((1,), (1,)), ((), ()))
TN_DIMS = (((0,), (0,)), ((), ()))


def iota(shape, axis):
    return lax.broadcasted_iota(I32, shape, axis)


def dot(a, b):
    return jnp.dot(a, b, preferred_element_type=F32)


def group_transpose(x):
    shape = x.shape
    sub, grp = iota(shape, 1), iota(shape, 2) >> 4
    for s in (1, 2, 4):
        sub_bit, lane_bit = (sub & s) != 0, (grp & s) != 0
        up = pltpu.roll(pltpu.roll(x, 8 - s, 1), 16 * s, 2)
        down = pltpu.roll(pltpu.roll(x, s, 1), 128 - 16 * s, 2)
        x = jnp.where(sub_bit == lane_bit, x, jnp.where(lane_bit, up, down))
    return x


def split(x):
    low = x - x.astype(BF16).astype(F32)
    return jnp.concatenate([x, low], axis=0).astype(BF16)


def in_time(pair, x):
    n = x.shape[0]
    high = x.astype(BF16)
    low = (x - high.astype(F32)).astype(BF16)
    out = dot(pair[0:n, :], jnp.concatenate([high, low], axis=1))
    return out[:, 0:128] + out[:, 128:256] + dot(pair[n : 2 * n, :], high)


def kernel(
    fb_in, ft_in, w_in, y_in, list_in, count_in, jac_in, prior_in, factor_in,
    x_out, r_out,
    jac, prior, factor, factor_t, slots, metas, order, rho_slot, picked, xs, rbuf, msend, mrecv, jw,
    psend, sig, cov, key, wgt, wy, uval, ubuf, vec,
    ss, gs, scal, scal_in, fsend, fbuf, ptmp,
    entered, in_sem, s_sem, ms_sem, r_sem, m_sem, ps_sem, p_sem, us_sem, u_sem, cs_sem, c_sem, fs_sem, f_sem,
):
    r, m = lax.axis_index("region"), lax.axis_index("tm")
    y, x, z, c = r // 4, r % 4, m // 2, m % 2

    def region_at(dy, dx):
        return ((y + dy) % 4) * 4 + (x + dx) % 4

    def tm_at(d):
        return ((z + d // 2) % 4) * 2 + (c + d) % 2

    jac_copy = pltpu.make_async_copy(jac_in, jac, in_sem.at[0])
    prior_copy = pltpu.make_async_copy(prior_in, prior, in_sem.at[1])
    factor_copy = pltpu.make_async_copy(factor_in, factor, in_sem.at[2])
    jac_copy.start()
    prior_copy.start()
    factor_copy.start()

    barrier = pltpu.get_barrier_semaphore()

    def greet_group(d, carry):
        pl.semaphore_signal(barrier, inc=1, device_id=(r, tm_at(d)), device_id_type=MESH)
        return carry

    def greet_region(i, carry):
        pl.semaphore_signal(barrier, inc=1, device_id=(region_at(i // 4, i % 4), m), device_id_type=MESH)
        return carry

    lax.fori_loop(1, 16, greet_region, 0)
    lax.fori_loop(1, 8, greet_group, 0)

    def as_row(ref):
        return ref[...].reshape(1, -1)

    blocks, starts = as_row(fb_in), as_row(ft_in)
    window = (starts * 1171) >> 16
    offset = starts - 56 * window
    named = jnp.where(iota((1, 512), 1) < count_in[0], as_row(list_in), -1)
    high = jnp.where(iota((32, 512), 0) == (named >> 5), 1.0, 0.0).astype(BF16)
    low = jnp.where(iota((32, 512), 0) == (named & 31), 1.0, 0.0).astype(BF16)
    table = lax.dot_general(high, low, NT_DIMS, preferred_element_type=F32).astype(BF16)
    sub, pool = iota((32, 768), 0), iota((32, 768), 1)
    table = dot(table, jnp.where(sub == (pool & 31), 1.0, 0.0).astype(BF16))
    kept = jnp.sum(jnp.where(sub == (pool >> 5), table, 0.0), axis=0, keepdims=True)
    target = (blocks >> 3) * 8 + window
    before = jnp.where(
        (iota((128, 256), 0) < iota((128, 256), 1)), 1.0, 0.0
    ).astype(BF16)
    ranks, carried = [], jnp.zeros((128, 128), F32)
    for i in range(6):
        part = slice(i * 128, i * 128 + 128)
        chosen = jnp.where((iota((128, 128), 0) == target[:, part]) & (kept[:, part] > 0.5), 1.0, 0.0)
        counts = dot(chosen.astype(BF16), before)
        ranks.append(jnp.sum(chosen * (counts[:, 0:128] + carried), axis=0, keepdims=True))
        carried = carried + counts[:, 128:256]
    rank = jnp.concatenate(ranks, axis=1)
    slots[...] = jnp.where(kept > 0.5, target * 6 + rank.astype(I32), -1)

    row = iota((16, 768), 0)
    meta = jnp.where(row == 0, (blocks & 7).astype(F32), 0.0)
    meta = jnp.where(row == 1, offset.astype(F32), meta)
    meta = jnp.where(row == 2, as_row(w_in).astype(F32), meta)
    meta = jnp.where(row == 3, as_row(y_in).astype(F32), meta)
    meta = jnp.where(row == 4, (offset & 15).astype(F32), meta)
    metas[...] = meta.astype(BF16)

    pl.semaphore_wait(barrier, 22)

    def vouch(d, carry):
        pl.semaphore_signal(entered, inc=1, device_id=(r, tm_at(d)), device_id_type=MESH)
        return carry

    lax.fori_loop(1, 8, vouch, 0)

    prior_copy.wait()
    ptmp[...] = group_transpose(prior[...])
    for i in range(8):
        psend[i] = ptmp[:, i, :]
    sig[m] = psend[m]

    jac_copy.wait()
    pl.semaphore_wait(entered, 7)

    def send_prior(d, carry):
        t = tm_at(d)
        pltpu.make_async_remote_copy(
            src_ref=psend.at[t], dst_ref=sig.at[m], send_sem=ps_sem, recv_sem=p_sem,
            device_id=(r, t), device_id_type=MESH,
        ).start()
        return carry

    lax.fori_loop(1, 8, send_prior, 0)
    own = m
    lane = iota((1, 128), 1)
    lanes = iota((16, 128), 1) >> 4

    def deliver(g, carry):
        to = [region_at(g // 4 + 2 * k, g % 4 + 2 * k) for k in range(2)]
        which = jnp.concatenate(
            [jnp.where(iota((48, 768), 0) + t * 48 == slots[...], 1.0, 0.0) for t in to], axis=0
        ).astype(BF16)
        meta = lax.dot_general(metas[...], which, NT_DIMS, preferred_element_type=F32)
        rho_slot[...] = lax.dot_general(
            meta.astype(BF16), jnp.where(iota((16, 128), 0) == 4, 1.0, 0.0).astype(BF16), TN_DIMS,
            preferred_element_type=F32,
        ).astype(I32)
        meta = jnp.concatenate([meta, jnp.zeros((16, 32), F32)], axis=1)
        for k in range(2):
            part = meta if k == 0 else pltpu.roll(meta, 128 - 48, 1)
            msend[g * 2 + k, 0:1, :] = jnp.where(
                lane < 64, part[0:1] * 64.0 + part[1:2], pltpu.roll(part[2:3], 64, 1)
            )
            msend[g * 2 + k, 1:2, :] = part[2:3] * part[3:4]
        for l in range(0, 2048, 256):
            picked[:, l : l + 256] = dot(which, jac[:, l : l + 256])
        for k in range(2):

            def turn(i, carry, k=k):
                rows = pl.ds(pl.multiple_of(k * 48 + i * 16, 16), 16)
                out = pl.ds(pl.multiple_of(i * 16, 16), 16)
                rho = rho_slot[rows, :]
                parts = [picked[rows, l * 128 : (l + 1) * 128] for l in range(16)]
                for s in (1, 2, 4, 8):
                    bit = (rho & s) != 0
                    parts = [jnp.where(bit, parts[(l - s) % 16], parts[l]) for l in range(16)]
                for half in range(2):
                    v = parts[half * 8 : half * 8 + 8]
                    for s in (1, 2, 4):
                        bit = (lanes & s) != 0
                        new = list(v)
                        for n in range(8):
                            if n & s == 0:
                                new[n] = jnp.where(bit, pltpu.roll(v[n + s], 16 * s, 1), v[n])
                                new[n + s] = jnp.where(bit, v[n + s], pltpu.roll(v[n], 128 - 16 * s, 1))
                        v = new
                    for n in range(8):
                        xs[g * 16 + k * 8 + n, out, half * 128 : (half + 1) * 128] = v[n].astype(BF16)
                return carry

            lax.fori_loop(0, 3, turn, 0)

        def send(k, d):
            t = tm_at((3 * d) % 8)
            here = g * 16 + k * 8 + m
            pltpu.make_async_remote_copy(
                src_ref=msend.at[g * 2 + k], dst_ref=mrecv.at[here], send_sem=ms_sem, recv_sem=m_sem.at[g],
                device_id=(to[k], t), device_id_type=MESH,
            ).start()
            pltpu.make_async_remote_copy(
                src_ref=xs.at[g * 16 + k * 8 + t], dst_ref=rbuf.at[here], send_sem=s_sem, recv_sem=r_sem.at[g],
                device_id=(to[k], t), device_id_type=MESH,
            ).start()

        def send_two(d, carry):
            send(0, d)
            send(1, d)
            return carry

        @pl.when(g > 0)
        def _():
            send(0, 0)

        send(1, 0)
        lax.fori_loop(1, 8, send_two, 0)
        return carry

    lax.fori_loop(0, 8, deliver, 0)
    local_rows = pltpu.make_async_copy(xs.at[own], rbuf.at[own], r_sem.at[0])
    local_meta = pltpu.make_async_copy(msend.at[0], mrecv.at[own], m_sem.at[0])
    local_rows.start()
    local_meta.start()

    factor_copy.wait()
    product = lax.dot_general(factor[...], factor[...], NT_DIMS, precision=HIGH, preferred_element_type=F32)
    for ref, value in ((cov, product), (factor_t, jnp.transpose(factor[...]))):
        ref[0:448, :] = value.astype(BF16)
        ref[448:896, :] = (value - value.astype(BF16).astype(F32)).astype(BF16)
    oi = iota((768, 768), 0)
    order[...] = jnp.where(iota((768, 768), 1) == (oi & 15) * 48 + (oi >> 4), 1.0, 0.0).astype(BF16)

    lane_lag = iota((16, 256), 1) >> 4

    def receive(g, carry):
        batch = pl.ds(g * 16, 16)
        pltpu.make_async_copy(mrecv.at[batch], mrecv.at[batch], m_sem.at[g]).wait()
        pltpu.make_async_copy(rbuf.at[batch], rbuf.at[batch], r_sem.at[g]).wait()
        rows = dot(order[...], rbuf[batch].reshape(768, 256))
        rho = mrecv[batch, 0, :].astype(I32) & 15
        for k in range(48):
            tile = rows[k * 16 : k * 16 + 16]
            later = lane_lag < rho[:, k : k + 1]
            at = pl.ds(pl.multiple_of((k % 6) * 128 + g * 16, 16), 16)
            jw[k // 6, at, 0:256] = jnp.where(later, 0.0, tile).astype(BF16)
            jw[k // 6, at, 256:512] = jnp.where(later, tile, 0.0).astype(BF16)
        return carry

    lax.fori_loop(0, 8, receive, 0)

    first = jnp.transpose(mrecv[:, 0, :])
    second = jnp.transpose(mrecv[:, 1, :])
    code = first[0:48].astype(I32)
    key[...] = ((code & 63) >> 4) * 8 + (code >> 6)
    wgt[...] = first[64:112]
    wy[...] = second[0:48]
    pltpu.make_async_copy(sig.at[pl.ds(0, 7)], sig.at[pl.ds(0, 7)], p_sem).wait()

    rows24 = iota((24, 128), 0)

    def spread(values, ready):
        def one(w, carry):
            cols = []
            for j in range(6):
                at = pl.ds(w * 6 + j, 1)
                cols.append(jnp.where(rows24 == key[at, :], values[at, :], 0.0))
            out = dot(split(jnp.concatenate(cols, axis=1)), jw[w])
            out = out[:24] + out[24:]
            for a in range(4):
                for h in range(2 if a < 3 else 1):
                    val = None
                    if a < 3:
                        val = out[8 * a : 8 * a + 8, h * 128 : h * 128 + 128]
                    if a > 0:
                        more = out[8 * a - 8 : 8 * a, 256 + h * 128 : 384 + h * 128]
                        val = more if val is None else val + more
                    ss[w * 7 + 2 * a + h] = val
            return carry

        for half in range(2):
            ready(half)
            [one(w, 0) for w in range(half * 4, half * 4 + 4)]
        return group_transpose(ss[...]).reshape(448, 128) * sig[...].reshape(448, 128)

    def observe(g_field, phase):
        h_field = sig[...].reshape(448, 128) * in_time(cov, g_field)
        ss[...] = group_transpose(h_field.reshape(56, 8, 128))

        def one(w, carry):
            rows = []
            zero = jnp.zeros((8, 128), F32)
            for a in range(3):
                cells = [ss[w * 7 + 2 * a + h] for h in range(2)]
                for h in range(2):
                    cells.append(ss[w * 7 + 2 * a + 2 + h] if 2 * a + 2 + h < 7 else zero)
                rows.append(jnp.concatenate(cells, axis=1))
            v = lax.dot_general(split(jnp.concatenate(rows, axis=0)), jw[w], NT_DIMS, preferred_element_type=F32)
            v = v[:24] + v[24:]
            for j in range(6):
                uval[phase, pl.ds(w * 6 + j, 1), :] = jnp.sum(
                    jnp.where(rows24 == key[pl.ds(w * 6 + j, 1), :], v[:, j * 128 : (j + 1) * 128], 0.0),
                    axis=0, keepdims=True,
                )
            return carry

        for half in range(2):
            [one(w, 0) for w in range(half * 4, half * 4 + 4)]
            mine = uval.at[phase, pl.ds(half * 24, 24)]

            def send_values(d, carry, half=half, mine=mine):
                t = tm_at(d)
                pltpu.make_async_remote_copy(
                    src_ref=mine, dst_ref=ubuf.at[phase, half, m],
                    send_sem=us_sem.at[phase, half], recv_sem=u_sem.at[phase, half],
                    device_id=(r, t), device_id_type=MESH,
                ).start()
                return carry

            lax.fori_loop(1, 8, send_values, 0)
            ubuf[phase, half, m] = uval[phase, half * 24 : half * 24 + 24, :]

    def collect(phase):
        def ready(half):
            seven = ubuf.at[phase, half, pl.ds(0, 7)]
            pltpu.make_async_copy(seven, seven, u_sem.at[phase, half]).wait()
            total = ubuf[phase, half, 0]
            for i in range(1, 8):
                total = total + ubuf[phase, half, i]
            rows = slice(half * 24, half * 24 + 24)
            weighted = wgt[rows, :] * total
            vec[phase, rows, :] = weighted
            if phase == 0:
                terms = (wy[rows, :] * total, weighted * total)
            else:
                terms = (vec[0, rows, :] * total, weighted * total)
            for i, term in enumerate(terms):
                term = jnp.sum(term, axis=0, keepdims=True)
                at = slice(2 * phase + i, 2 * phase + i + 1)
                scal[at, :] = term if half == 0 else scal[at, :] + term

        return ready

    def send_field(k):
        fsend[k] = in_time(factor_t, gs[k]).reshape(8, 56, 128)

        def send(d, carry):
            t = tm_at(d)
            pltpu.make_async_remote_copy(
                src_ref=fsend.at[k, t], dst_ref=fbuf.at[k, m], send_sem=fs_sem.at[k], recv_sem=f_sem.at[k],
                device_id=(r, t), device_id_type=MESH,
            ).start()
            return carry

        lax.fori_loop(1, 8, send, 0)
        fbuf[k, m] = fsend[k, m]

    def wait_field(k):
        seven = fbuf.at[k, pl.ds(0, 7)]
        pltpu.make_async_copy(seven, seven, f_sem.at[k]).wait()

    scal[4:8, :] = jnp.zeros((4, 128), F32)
    gs[0] = spread(wy, lambda half: None)
    observe(gs[0], 0)
    send_field(0)
    gs[1] = spread(vec.at[0], collect(0))
    observe(gs[1], 1)
    send_field(1)
    gs[2] = spread(vec.at[1], collect(1))
    send_field(2)

    scal_in[r] = scal[...]

    def send_scal(i, carry):
        pltpu.make_async_remote_copy(
            src_ref=scal, dst_ref=scal_in.at[r], send_sem=cs_sem, recv_sem=c_sem,
            device_id=(region_at(i // 4, i % 4), m), device_id_type=MESH,
        ).start()
        return carry

    lax.fori_loop(1, 16, send_scal, 0)
    fifteen = scal_in.at[pl.ds(0, 15)]
    pltpu.make_async_copy(fifteen, fifteen, c_sem).wait()
    sums = scal_in[0]
    for i in range(1, 16):
        sums = sums + scal_in[i]
    sums = jnp.sum(sums, axis=1, keepdims=True)
    g00, g01, g11, g12 = (sums[i : i + 1, :] for i in range(4))
    a0 = g00 / (g00 + g01)
    rr1 = (1 - a0) * (1 - a0) * g00 - 2 * a0 * (1 - a0) * g01 + a0 * a0 * g11
    p, q = 1 - a0 + rr1 / g00, -a0
    a1 = rr1 / (p * p * g00 + p * (p + 2 * q) * g01 + q * (2 * p + q) * g11 + q * q * g12)
    wait_field(0)
    wait_field(1)
    for i in range(8):
        ptmp[:, i, :] = (a0 + a1 * p) * fbuf[0, i] + a1 * q * fbuf[1, i]
    x_out[...] = group_transpose(ptmp[...])
    for i in range(8):
        fbuf[0, i] = (1 - a0 - a1 * p) * fbuf[0, i] - (a0 + a1 * (p + q)) * fbuf[1, i]
    wait_field(2)
    for i in range(8):
        ptmp[:, i, :] = fbuf[0, i] - a1 * q * fbuf[2, i]
    r_out[...] = group_transpose(ptmp[...])

    all_rows, all_meta = xs.at[pl.ds(0, 127)], mrecv.at[pl.ds(0, 127)]
    pltpu.make_async_copy(all_rows, all_rows, s_sem).wait()
    pltpu.make_async_copy(all_meta, all_meta, ms_sem).wait()
    seven = sig.at[pl.ds(0, 7)]
    pltpu.make_async_copy(seven, seven, ps_sem).wait()
    for phase in range(2):
        for half in range(2):
            seven = ubuf.at[phase, half, pl.ds(0, 7)]
            pltpu.make_async_copy(seven, seven, us_sem.at[phase, half]).wait()
    pltpu.make_async_copy(fifteen, fifteen, cs_sem).wait()
    for k in range(3):
        seven = fbuf.at[k, pl.ds(0, 7)]
        pltpu.make_async_copy(seven, seven, fs_sem.at[k]).wait()


def hand_on(x_in, r_in, x_out, r_out):
    x_out[...] = x_in[...]
    r_out[...] = r_in[...]


def local(jacobian, foot_block, foot_time, obs_weight, misfit, kept_list, kept_count, prior_std, time_factor):
    field = jax.ShapeDtypeStruct(prior_std.shape, F32)
    vmem = pl.BlockSpec(memory_space=pltpu.VMEM)
    hbm = pl.BlockSpec(memory_space=pltpu.HBM)
    dma = pltpu.SemaphoreType.DMA
    fields = pl.pallas_call(
        kernel,
        out_shape=(field, field),
        in_specs=[vmem] * 5 + [pl.BlockSpec(memory_space=pltpu.SMEM)] + [hbm] * 3,
        out_specs=(vmem, vmem),
        scratch_shapes=[
            pltpu.VMEM((768, 2048), BF16),
            pltpu.VMEM((56, 8, 128), F32),
            pltpu.VMEM((448, 448), F32),
            pltpu.VMEM((896, 448), BF16),
            pltpu.VMEM((1, 768), I32),
            pltpu.VMEM((16, 768), BF16),
            pltpu.VMEM((768, 768), BF16),
            pltpu.VMEM((96, 128), I32),
            pltpu.VMEM((96, 2048), F32),
            pltpu.VMEM((128, 48, 256), BF16),
            pltpu.VMEM((128, 48, 256), BF16),
            pltpu.VMEM((16, 2, 128), F32),
            pltpu.VMEM((128, 2, 128), F32),
            pltpu.VMEM((8, 768, 512), BF16),
            pltpu.VMEM((8, 56, 128), F32),
            pltpu.VMEM((8, 56, 128), F32),
            pltpu.VMEM((896, 448), BF16),
            pltpu.VMEM((48, 128), I32),
            pltpu.VMEM((48, 128), F32),
            pltpu.VMEM((48, 128), F32),
            pltpu.VMEM((2, 48, 128), F32),
            pltpu.VMEM((2, 2, 8, 24, 128), F32),
            pltpu.VMEM((2, 48, 128), F32),
            pltpu.VMEM((56, 8, 128), F32),
            pltpu.VMEM((3, 448, 128), F32),
            pltpu.VMEM((8, 128), F32),
            pltpu.VMEM((16, 8, 128), F32),
            pltpu.VMEM((3, 8, 56, 128), F32),
            pltpu.VMEM((3, 8, 56, 128), F32),
            pltpu.VMEM((56, 8, 128), F32),
            pltpu.SemaphoreType.REGULAR, dma((3,)), dma, dma, dma((8,)), dma((8,)), dma, dma, dma((2, 2)), dma((2, 2)), dma, dma, dma((3,)), dma((3,)),
        ],
        compiler_params=pltpu.CompilerParams(
            collective_id=0, has_side_effects=True, vmem_limit_bytes=60 * 2**20
        ),
    )(foot_block, foot_time, obs_weight, misfit, kept_list, kept_count, jacobian, prior_std, time_factor)
    return pl.pallas_call(
        hand_on, out_shape=(field, field), in_specs=[vmem, vmem], out_specs=(vmem, vmem)
    )(*fields)


def solution(mesh):
    rows = P(("region", "tm"))
    return jax.shard_map(
        local,
        mesh=mesh,
        in_specs=(
            P(("region", "tm"), None), rows, rows, rows, rows, rows, rows, P("tm", "region", None), P(),
        ),
        out_specs=(P("tm", "region", None), P("tm", "region", None)),
        check_vma=False,
    )
```

```python
import jax
import jax.numpy as jnp
from jax import lax
from jax.experimental import pallas as pl
from jax.experimental.pallas import tpu as pltpu
from jax.sharding import PartitionSpec as P

MESH = pl.DeviceIdType.MESH
HIGH = lax.Precision.HIGHEST
F32 = jnp.float32
BF16 = jnp.bfloat16
I32 = jnp.int32

NT_DIMS = (((1,), (1,)), ((), ()))
TN_DIMS = (((0,), (0,)), ((), ()))


def iota(shape, axis):
    return lax.broadcasted_iota(I32, shape, axis)


def dot(a, b):
    return jnp.dot(a, b, preferred_element_type=F32)


def group_transpose(x):
    shape = x.shape
    sub, grp = iota(shape, 1), iota(shape, 2) >> 4
    for s in (1, 2, 4):
        sub_bit, lane_bit = (sub & s) != 0, (grp & s) != 0
        up = pltpu.roll(pltpu.roll(x, 8 - s, 1), 16 * s, 2)
        down = pltpu.roll(pltpu.roll(x, s, 1), 128 - 16 * s, 2)
        x = jnp.where(sub_bit == lane_bit, x, jnp.where(lane_bit, up, down))
    return x


def split(x):
    low = x - x.astype(BF16).astype(F32)
    return jnp.concatenate([x, low], axis=0).astype(BF16)


def in_time(pair, x):
    n = x.shape[0]
    high = x.astype(BF16)
    low = (x - high.astype(F32)).astype(BF16)
    out = dot(pair[0:n, :], jnp.concatenate([high, low], axis=1))
    return out[:, 0:128] + out[:, 128:256] + dot(pair[n : 2 * n, :], high)


def kernel(
    fb_in, ft_in, w_in, y_in, list_in, count_in, jac_in, prior_in, factor_in,
    x_out, r_out,
    jac, prior, factor, factor_t, slots, metas, order, rho_slot, picked, xs, rbuf, msend, mrecv, jw, jwt,
    psend, sig, cov, key, wgt, wy, uval, ubuf, vec,
    ss, gs, scal, scal_in, fsend, fbuf, ptmp,
    entered, in_sem, s_sem, ms_sem, r_sem, m_sem, ps_sem, p_sem, us_sem, u_sem, cs_sem, c_sem, fs_sem, f_sem,
):
    r, m = lax.axis_index("region"), lax.axis_index("tm")
    y, x, z, c = r // 4, r % 4, m // 2, m % 2

    def region_at(dy, dx):
        return ((y + dy) % 4) * 4 + (x + dx) % 4

    def tm_at(d):
        return ((z + d // 2) % 4) * 2 + (c + d) % 2

    jac_copy = pltpu.make_async_copy(jac_in, jac, in_sem.at[0])
    prior_copy = pltpu.make_async_copy(prior_in, prior, in_sem.at[1])
    factor_copy = pltpu.make_async_copy(factor_in, factor, in_sem.at[2])
    jac_copy.start()
    prior_copy.start()
    factor_copy.start()

    barrier = pltpu.get_barrier_semaphore()

    def greet_group(d, carry):
        pl.semaphore_signal(barrier, inc=1, device_id=(r, tm_at(d)), device_id_type=MESH)
        return carry

    def greet_region(i, carry):
        pl.semaphore_signal(barrier, inc=1, device_id=(region_at(i // 4, i % 4), m), device_id_type=MESH)
        return carry

    lax.fori_loop(1, 16, greet_region, 0)
    lax.fori_loop(1, 8, greet_group, 0)

    def as_row(ref):
        return ref[...].reshape(1, -1)

    blocks, starts = as_row(fb_in), as_row(ft_in)
    window = (starts * 1171) >> 16
    offset = starts - 56 * window
    named = jnp.where(iota((1, 512), 1) < count_in[0], as_row(list_in), -1)
    high = jnp.where(iota((32, 512), 0) == (named >> 5), 1.0, 0.0).astype(BF16)
    low = jnp.where(iota((32, 512), 0) == (named & 31), 1.0, 0.0).astype(BF16)
    table = lax.dot_general(high, low, NT_DIMS, preferred_element_type=F32).astype(BF16)
    sub, pool = iota((32, 768), 0), iota((32, 768), 1)
    table = dot(table, jnp.where(sub == (pool & 31), 1.0, 0.0).astype(BF16))
    kept = jnp.sum(jnp.where(sub == (pool >> 5), table, 0.0), axis=0, keepdims=True)
    target = (blocks >> 3) * 8 + window
    before = jnp.where(
        (iota((128, 256), 0) < iota((128, 256), 1)), 1.0, 0.0
    ).astype(BF16)
    ranks, carried = [], jnp.zeros((128, 128), F32)
    for i in range(6):
        part = slice(i * 128, i * 128 + 128)
        chosen = jnp.where((iota((128, 128), 0) == target[:, part]) & (kept[:, part] > 0.5), 1.0, 0.0)
        counts = dot(chosen.astype(BF16), before)
        ranks.append(jnp.sum(chosen * (counts[:, 0:128] + carried), axis=0, keepdims=True))
        carried = carried + counts[:, 128:256]
    rank = jnp.concatenate(ranks, axis=1)
    slots[...] = jnp.where(kept > 0.5, target * 6 + rank.astype(I32), -1)

    row = iota((16, 768), 0)
    meta = jnp.where(row == 0, (blocks & 7).astype(F32), 0.0)
    meta = jnp.where(row == 1, offset.astype(F32), meta)
    meta = jnp.where(row == 2, as_row(w_in).astype(F32), meta)
    meta = jnp.where(row == 3, as_row(y_in).astype(F32), meta)
    meta = jnp.where(row == 4, (offset & 15).astype(F32), meta)
    metas[...] = meta.astype(BF16)

    pl.semaphore_wait(barrier, 22)

    def vouch(d, carry):
        pl.semaphore_signal(entered, inc=1, device_id=(r, tm_at(d)), device_id_type=MESH)
        return carry

    lax.fori_loop(1, 8, vouch, 0)

    prior_copy.wait()
    ptmp[...] = group_transpose(prior[...])
    for i in range(8):
        psend[i] = ptmp[:, i, :]
    sig[m] = psend[m]

    jac_copy.wait()
    pl.semaphore_wait(entered, 7)

    def send_prior(d, carry):
        t = tm_at(d)
        pltpu.make_async_remote_copy(
            src_ref=psend.at[t], dst_ref=sig.at[m], send_sem=ps_sem, recv_sem=p_sem,
            device_id=(r, t), device_id_type=MESH,
        ).start()
        return carry

    lax.fori_loop(1, 8, send_prior, 0)
    own = m
    lane = iota((1, 128), 1)
    lanes = iota((16, 128), 1) >> 4

    def deliver(g, carry):
        to = [region_at(g // 4 + 2 * k, g % 4 + 2 * k) for k in range(2)]
        which = jnp.concatenate(
            [jnp.where(iota((48, 768), 0) + t * 48 == slots[...], 1.0, 0.0) for t in to], axis=0
        ).astype(BF16)
        meta = lax.dot_general(metas[...], which, NT_DIMS, preferred_element_type=F32)
        rho_slot[...] = lax.dot_general(
            meta.astype(BF16), jnp.where(iota((16, 128), 0) == 4, 1.0, 0.0).astype(BF16), TN_DIMS,
            preferred_element_type=F32,
        ).astype(I32)
        meta = jnp.concatenate([meta, jnp.zeros((16, 32), F32)], axis=1)
        for k in range(2):
            part = meta if k == 0 else pltpu.roll(meta, 128 - 48, 1)
            msend[g * 2 + k, 0:1, :] = jnp.where(
                lane < 64, part[0:1] * 64.0 + part[1:2], pltpu.roll(part[2:3], 64, 1)
            )
            msend[g * 2 + k, 1:2, :] = part[2:3] * part[3:4]
        for l in range(0, 2048, 256):
            picked[:, l : l + 256] = dot(which, jac[:, l : l + 256])
        for k in range(2):

            def turn(i, carry, k=k):
                rows = pl.ds(pl.multiple_of(k * 48 + i * 16, 16), 16)
                out = pl.ds(pl.multiple_of(i * 16, 16), 16)
                rho = rho_slot[rows, :]
                parts = [picked[rows, l * 128 : (l + 1) * 128] for l in range(16)]
                for s in (1, 2, 4, 8):
                    bit = (rho & s) != 0
                    parts = [jnp.where(bit, parts[(l - s) % 16], parts[l]) for l in range(16)]
                for half in range(2):
                    v = parts[half * 8 : half * 8 + 8]
                    for s in (1, 2, 4):
                        bit = (lanes & s) != 0
                        new = list(v)
                        for n in range(8):
                            if n & s == 0:
                                new[n] = jnp.where(bit, pltpu.roll(v[n + s], 16 * s, 1), v[n])
                                new[n + s] = jnp.where(bit, v[n + s], pltpu.roll(v[n], 128 - 16 * s, 1))
                        v = new
                    for n in range(8):
                        xs[g * 16 + k * 8 + n, out, half * 128 : (half + 1) * 128] = v[n].astype(BF16)
                return carry

            for i in range(3):
                turn(i, 0)

        def send(k, d):
            t = tm_at((3 * d + 4 * k) % 8)
            here = g * 16 + k * 8 + m
            pltpu.make_async_remote_copy(
                src_ref=msend.at[g * 2 + k], dst_ref=mrecv.at[here], send_sem=ms_sem, recv_sem=m_sem.at[g],
                device_id=(to[k], t), device_id_type=MESH,
            ).start()
            pltpu.make_async_remote_copy(
                src_ref=xs.at[g * 16 + k * 8 + t], dst_ref=rbuf.at[here], send_sem=s_sem, recv_sem=r_sem.at[g],
                device_id=(to[k], t), device_id_type=MESH,
            ).start()

        def send_two(d, carry):
            send(0, d)
            send(1, d)
            return carry

        @pl.when(g > 0)
        def _():
            send(0, 0)

        send(1, 0)
        lax.fori_loop(1, 8, send_two, 0)
        return carry

    lax.fori_loop(0, 8, deliver, 0)
    local_rows = pltpu.make_async_copy(xs.at[own], rbuf.at[own], r_sem.at[0])
    local_meta = pltpu.make_async_copy(msend.at[0], mrecv.at[own], m_sem.at[0])
    local_rows.start()
    local_meta.start()

    factor_copy.wait()
    product = lax.dot_general(factor[...], factor[...], NT_DIMS, precision=HIGH, preferred_element_type=F32)
    for ref, value in ((cov, product), (factor_t, jnp.transpose(factor[...]))):
        ref[0:448, :] = value.astype(BF16)
        ref[448:896, :] = (value - value.astype(BF16).astype(F32)).astype(BF16)
    oi = iota((768, 768), 0)
    order[...] = jnp.where(iota((768, 768), 1) == (oi & 15) * 48 + (oi >> 4), 1.0, 0.0).astype(BF16)

    lane_lag = iota((16, 256), 1) >> 4

    def receive(g, carry):
        batch = pl.ds(g * 16, 16)
        pltpu.make_async_copy(mrecv.at[batch], mrecv.at[batch], m_sem.at[g]).wait()
        pltpu.make_async_copy(rbuf.at[batch], rbuf.at[batch], r_sem.at[g]).wait()
        rows = dot(order[...], rbuf[batch].reshape(768, 256))
        rho = mrecv[batch, 0, :].astype(I32) & 15
        for k in range(48):
            tile = rows[k * 16 : k * 16 + 16]
            later = lane_lag < rho[:, k : k + 1]
            at = pl.ds(pl.multiple_of((k % 6) * 128 + g * 16, 16), 16)
            jw[k // 6, at, 0:256] = jnp.where(later, 0.0, tile).astype(BF16)
            jw[k // 6, at, 256:512] = jnp.where(later, tile, 0.0).astype(BF16)
        return carry

    lax.fori_loop(0, 8, receive, 0)

    first = jnp.transpose(mrecv[:, 0, :])
    second = jnp.transpose(mrecv[:, 1, :])
    code = first[0:48].astype(I32)
    key[...] = ((code & 63) >> 4) * 8 + (code >> 6)
    wgt[...] = first[64:112]
    wy[...] = second[0:48]
    pltpu.make_async_copy(sig.at[pl.ds(0, 7)], sig.at[pl.ds(0, 7)], p_sem).wait()

    rows24 = iota((24, 128), 0)

    def spread(values, ready):
        def one(w, carry):
            cols = []
            for j in range(6):
                at = pl.ds(w * 6 + j, 1)
                cols.append(jnp.where(rows24 == key[at, :], values[at, :], 0.0))
            out = dot(split(jnp.concatenate(cols, axis=1)), jw[w])
            out = out[:24] + out[24:]
            for a in range(4):
                for h in range(2 if a < 3 else 1):
                    val = None
                    if a < 3:
                        val = out[8 * a : 8 * a + 8, h * 128 : h * 128 + 128]
                    if a > 0:
                        more = out[8 * a - 8 : 8 * a, 256 + h * 128 : 384 + h * 128]
                        val = more if val is None else val + more
                    ss[w * 7 + 2 * a + h] = val
            return carry

        for half in range(2):
            ready(half)
            [one(w, 0) for w in range(half * 4, half * 4 + 4)]
        return group_transpose(ss[...]).reshape(448, 128) * sig[...].reshape(448, 128)

    def observe(g_field, phase):
        h_field = sig[...].reshape(448, 128) * in_time(cov, g_field)
        ss[...] = group_transpose(h_field.reshape(56, 8, 128))

        def one(w, carry):
            rows = []
            zero = jnp.zeros((8, 128), F32)
            for a in range(3):
                cells = [ss[w * 7 + 2 * a + h] for h in range(2)]
                for h in range(2):
                    cells.append(ss[w * 7 + 2 * a + 2 + h] if 2 * a + 2 + h < 7 else zero)
                rows.append(jnp.concatenate(cells, axis=1))
            if phase == 0:
                turned = jnp.transpose(jw[w])
                jwt[w] = turned
            else:
                turned = jwt[w]
            v = dot(split(jnp.concatenate(rows, axis=0)), turned)
            v = v[:24] + v[24:]
            for j in range(6):
                uval[phase, pl.ds(w * 6 + j, 1), :] = jnp.sum(
                    jnp.where(rows24 == key[pl.ds(w * 6 + j, 1), :], v[:, j * 128 : (j + 1) * 128], 0.0),
                    axis=0, keepdims=True,
                )
            return carry

        for half in range(2):
            [one(w, 0) for w in range(half * 4, half * 4 + 4)]
            mine = uval.at[phase, pl.ds(half * 24, 24)]

            def send_values(d, carry, half=half, mine=mine):
                t = tm_at(d)
                pltpu.make_async_remote_copy(
                    src_ref=mine, dst_ref=ubuf.at[phase, half, m],
                    send_sem=us_sem.at[phase, half], recv_sem=u_sem.at[phase, half],
                    device_id=(r, t), device_id_type=MESH,
                ).start()
                return carry

            for d in range(1, 8):
                send_values(d, 0)
            ubuf[phase, half, m] = uval[phase, half * 24 : half * 24 + 24, :]

    def collect(phase):
        def ready(half):
            seven = ubuf.at[phase, half, pl.ds(0, 7)]
            pltpu.make_async_copy(seven, seven, u_sem.at[phase, half]).wait()
            total = ubuf[phase, half, 0]
            for i in range(1, 8):
                total = total + ubuf[phase, half, i]
            rows = slice(half * 24, half * 24 + 24)
            weighted = wgt[rows, :] * total
            vec[phase, rows, :] = weighted
            if phase == 0:
                terms = (wy[rows, :] * total, weighted * total)
            else:
                terms = (vec[0, rows, :] * total, weighted * total)
            for i, term in enumerate(terms):
                term = jnp.sum(term, axis=0, keepdims=True)
                at = slice(2 * phase + i, 2 * phase + i + 1)
                scal[at, :] = term if half == 0 else scal[at, :] + term
            if phase == 1 and half == 1:
                send_sums()

        return ready

    def send_field(k):
        fsend[k] = in_time(factor_t, gs[k]).reshape(8, 56, 128)

        def send(d, carry):
            t = tm_at(d)
            pltpu.make_async_remote_copy(
                src_ref=fsend.at[k, t], dst_ref=fbuf.at[k, m], send_sem=fs_sem.at[k], recv_sem=f_sem.at[k],
                device_id=(r, t), device_id_type=MESH,
            ).start()
            return carry

        for d in range(1, 8):
            send(d, 0)
        fbuf[k, m] = fsend[k, m]

    def wait_field(k):
        seven = fbuf.at[k, pl.ds(0, 7)]
        pltpu.make_async_copy(seven, seven, f_sem.at[k]).wait()

    def send_sums():
        scal_in[r] = scal[...]
        for i in range(1, 16):
            pltpu.make_async_remote_copy(
                src_ref=scal, dst_ref=scal_in.at[r], send_sem=cs_sem, recv_sem=c_sem,
                device_id=(region_at(i // 4, i % 4), m), device_id_type=MESH,
            ).start()

    scal[4:8, :] = jnp.zeros((4, 128), F32)
    gs[0] = spread(wy, lambda half: None)
    observe(gs[0], 0)
    send_field(0)
    gs[1] = spread(vec.at[0], collect(0))
    observe(gs[1], 1)
    send_field(1)
    gs[2] = spread(vec.at[1], collect(1))
    send_field(2)

    fifteen = scal_in.at[pl.ds(0, 15)]
    pltpu.make_async_copy(fifteen, fifteen, c_sem).wait()
    sums = scal_in[0]
    for i in range(1, 16):
        sums = sums + scal_in[i]
    sums = jnp.sum(sums, axis=1, keepdims=True)
    g00, g01, g11, g12 = (sums[i : i + 1, :] for i in range(4))
    a0 = g00 / (g00 + g01)
    rr1 = (1 - a0) * (1 - a0) * g00 - 2 * a0 * (1 - a0) * g01 + a0 * a0 * g11
    p, q = 1 - a0 + rr1 / g00, -a0
    a1 = rr1 / (p * p * g00 + p * (p + 2 * q) * g01 + q * (2 * p + q) * g11 + q * q * g12)
    wait_field(0)
    wait_field(1)
    for i in range(8):
        ptmp[:, i, :] = (a0 + a1 * p) * fbuf[0, i] + a1 * q * fbuf[1, i]
    x_out[...] = group_transpose(ptmp[...])
    for i in range(8):
        fbuf[0, i] = (1 - a0 - a1 * p) * fbuf[0, i] - (a0 + a1 * (p + q)) * fbuf[1, i]
    wait_field(2)
    for i in range(8):
        ptmp[:, i, :] = fbuf[0, i] - a1 * q * fbuf[2, i]
    r_out[...] = group_transpose(ptmp[...])

    all_rows, all_meta = xs.at[pl.ds(0, 127)], mrecv.at[pl.ds(0, 127)]
    pltpu.make_async_copy(all_rows, all_rows, s_sem).wait()
    pltpu.make_async_copy(all_meta, all_meta, ms_sem).wait()
    seven = sig.at[pl.ds(0, 7)]
    pltpu.make_async_copy(seven, seven, ps_sem).wait()
    for phase in range(2):
        for half in range(2):
            seven = ubuf.at[phase, half, pl.ds(0, 7)]
            pltpu.make_async_copy(seven, seven, us_sem.at[phase, half]).wait()
    pltpu.make_async_copy(fifteen, fifteen, cs_sem).wait()
    for k in range(3):
        seven = fbuf.at[k, pl.ds(0, 7)]
        pltpu.make_async_copy(seven, seven, fs_sem.at[k]).wait()


def hand_on(x_in, r_in, x_out, r_out):
    x_out[...] = x_in[...]
    r_out[...] = r_in[...]


def local(jacobian, foot_block, foot_time, obs_weight, misfit, kept_list, kept_count, prior_std, time_factor):
    field = jax.ShapeDtypeStruct(prior_std.shape, F32)
    vmem = pl.BlockSpec(memory_space=pltpu.VMEM)
    hbm = pl.BlockSpec(memory_space=pltpu.HBM)
    dma = pltpu.SemaphoreType.DMA
    fields = pl.pallas_call(
        kernel,
        out_shape=(field, field),
        in_specs=[vmem] * 5 + [pl.BlockSpec(memory_space=pltpu.SMEM)] + [hbm] * 3,
        out_specs=(vmem, vmem),
        scratch_shapes=[
            pltpu.VMEM((768, 2048), BF16),
            pltpu.VMEM((56, 8, 128), F32),
            pltpu.VMEM((448, 448), F32),
            pltpu.VMEM((896, 448), BF16),
            pltpu.VMEM((1, 768), I32),
            pltpu.VMEM((16, 768), BF16),
            pltpu.VMEM((768, 768), BF16),
            pltpu.VMEM((96, 128), I32),
            pltpu.VMEM((96, 2048), F32),
            pltpu.VMEM((128, 48, 256), BF16),
            pltpu.VMEM((128, 48, 256), BF16),
            pltpu.VMEM((16, 2, 128), F32),
            pltpu.VMEM((128, 2, 128), F32),
            pltpu.VMEM((8, 768, 512), BF16),
            pltpu.VMEM((8, 512, 768), BF16),
            pltpu.VMEM((8, 56, 128), F32),
            pltpu.VMEM((8, 56, 128), F32),
            pltpu.VMEM((896, 448), BF16),
            pltpu.VMEM((48, 128), I32),
            pltpu.VMEM((48, 128), F32),
            pltpu.VMEM((48, 128), F32),
            pltpu.VMEM((2, 48, 128), F32),
            pltpu.VMEM((2, 2, 8, 24, 128), F32),
            pltpu.VMEM((2, 48, 128), F32),
            pltpu.VMEM((56, 8, 128), F32),
            pltpu.VMEM((3, 448, 128), F32),
            pltpu.VMEM((8, 128), F32),
            pltpu.VMEM((16, 8, 128), F32),
            pltpu.VMEM((3, 8, 56, 128), F32),
            pltpu.VMEM((3, 8, 56, 128), F32),
            pltpu.VMEM((56, 8, 128), F32),
            pltpu.SemaphoreType.REGULAR, dma((3,)), dma, dma, dma((8,)), dma((8,)), dma, dma, dma((2, 2)), dma((2, 2)), dma, dma, dma((3,)), dma((3,)),
        ],
        compiler_params=pltpu.CompilerParams(
            collective_id=0, has_side_effects=True, vmem_limit_bytes=60 * 2**20
        ),
    )(foot_block, foot_time, obs_weight, misfit, kept_list, kept_count, jacobian, prior_std, time_factor)
    return pl.pallas_call(
        hand_on, out_shape=(field, field), in_specs=[vmem, vmem], out_specs=(vmem, vmem)
    )(*fields)


def solution(mesh):
    rows = P(("region", "tm"))
    return jax.shard_map(
        local,
        mesh=mesh,
        in_specs=(
            P(("region", "tm"), None), rows, rows, rows, rows, rows, rows, P("tm", "region", None), P(),
        ),
        out_specs=(P("tm", "region", None), P("tm", "region", None)),
        check_vma=False,
    )
```

```python
import jax
import jax.numpy as jnp
from jax import lax
from jax.experimental import pallas as pl
from jax.experimental.pallas import tpu as pltpu
from jax.sharding import PartitionSpec as P

MESH = pl.DeviceIdType.MESH
HIGH = lax.Precision.HIGHEST
F32 = jnp.float32
BF16 = jnp.bfloat16
I32 = jnp.int32

NT_DIMS = (((1,), (1,)), ((), ()))
TN_DIMS = (((0,), (0,)), ((), ()))


def iota(shape, axis):
    return lax.broadcasted_iota(I32, shape, axis)


def dot(a, b):
    return jnp.dot(a, b, preferred_element_type=F32)


def group_transpose(x):
    shape = x.shape
    sub, grp = iota(shape, 1), iota(shape, 2) >> 4
    for s in (1, 2, 4):
        sub_bit, lane_bit = (sub & s) != 0, (grp & s) != 0
        up = pltpu.roll(pltpu.roll(x, 8 - s, 1), 16 * s, 2)
        down = up if s == 4 else pltpu.roll(pltpu.roll(x, s, 1), 128 - 16 * s, 2)
        x = jnp.where(sub_bit == lane_bit, x, jnp.where(lane_bit, up, down))
    return x


def split(x):
    low = x - x.astype(BF16).astype(F32)
    return jnp.concatenate([x, low], axis=0).astype(BF16)


def in_time(pair, x):
    n = x.shape[0]
    high = x.astype(BF16)
    low = (x - high.astype(F32)).astype(BF16)
    out = dot(pair[0:n, :], jnp.concatenate([high, low], axis=1))
    return out[:, 0:128] + out[:, 128:256] + dot(pair[n : 2 * n, :], high)


def kernel(
    fb_in, ft_in, w_in, y_in, list_in, count_in, jac_in, prior_in, factor_in,
    x_out, r_out,
    jac, prior, factor, factor_t, slots, metas, order, rho_slot, picked, xs, rbuf, msend, mrecv, jw, jwt,
    psend, sig, cov, key, wgt, wy, uval, ubuf, vec,
    ss, gs, scal, scal_in, fsend, fbuf, ptmp,
    entered, in_sem, s_sem, ms_sem, r_sem, m_sem, ps_sem, p_sem, us_sem, u_sem, cs_sem, c_sem, fs_sem, f_sem,
):
    r, m = lax.axis_index("region"), lax.axis_index("tm")
    y, x, z, c = r // 4, r % 4, m // 2, m % 2

    def region_at(dy, dx):
        return ((y + dy) % 4) * 4 + (x + dx) % 4

    def tm_at(d):
        return ((z + d // 2) % 4) * 2 + (c + d) % 2

    jac_copy = pltpu.make_async_copy(jac_in, jac, in_sem.at[0])
    prior_copy = pltpu.make_async_copy(prior_in, prior, in_sem.at[1])
    factor_copy = pltpu.make_async_copy(factor_in, factor, in_sem.at[2])
    jac_copy.start()
    prior_copy.start()
    factor_copy.start()

    barrier = pltpu.get_barrier_semaphore()

    def greet_group(d, carry):
        pl.semaphore_signal(barrier, inc=1, device_id=(r, tm_at(d)), device_id_type=MESH)
        return carry

    def greet_region(i, carry):
        pl.semaphore_signal(barrier, inc=1, device_id=(region_at(i // 4, i % 4), m), device_id_type=MESH)
        return carry

    lax.fori_loop(1, 16, greet_region, 0)
    lax.fori_loop(1, 8, greet_group, 0)

    def as_row(ref):
        return ref[...].reshape(1, -1)

    blocks, starts = as_row(fb_in), as_row(ft_in)
    window = (starts * 1171) >> 16
    offset = starts - 56 * window
    named = jnp.where(iota((1, 512), 1) < count_in[0], as_row(list_in), -1)
    high = jnp.where(iota((32, 512), 0) == (named >> 5), 1.0, 0.0).astype(BF16)
    low = jnp.where(iota((32, 512), 0) == (named & 31), 1.0, 0.0).astype(BF16)
    table = lax.dot_general(high, low, NT_DIMS, preferred_element_type=F32).astype(BF16)
    sub, pool = iota((32, 768), 0), iota((32, 768), 1)
    table = dot(table, jnp.where(sub == (pool & 31), 1.0, 0.0).astype(BF16))
    kept = jnp.sum(jnp.where(sub == (pool >> 5), table, 0.0), axis=0, keepdims=True)
    target = (blocks >> 3) * 8 + window
    before = jnp.where(
        (iota((128, 256), 0) < iota((128, 256), 1)), 1.0, 0.0
    ).astype(BF16)
    ranks, carried = [], jnp.zeros((128, 128), F32)
    for i in range(6):
        part = slice(i * 128, i * 128 + 128)
        chosen = jnp.where((iota((128, 128), 0) == target[:, part]) & (kept[:, part] > 0.5), 1.0, 0.0)
        counts = dot(chosen.astype(BF16), before)
        ranks.append(jnp.sum(chosen * (counts[:, 0:128] + carried), axis=0, keepdims=True))
        carried = carried + counts[:, 128:256]
    rank = jnp.concatenate(ranks, axis=1)
    slots[...] = jnp.where(kept > 0.5, target * 6 + rank.astype(I32), -1)

    row = iota((16, 768), 0)
    meta = jnp.where(row == 0, (blocks & 7).astype(F32), 0.0)
    meta = jnp.where(row == 1, offset.astype(F32), meta)
    meta = jnp.where(row == 2, as_row(w_in).astype(F32), meta)
    meta = jnp.where(row == 3, as_row(y_in).astype(F32), meta)
    meta = jnp.where(row == 4, (offset & 15).astype(F32), meta)
    metas[...] = meta.astype(BF16)

    pl.semaphore_wait(barrier, 22)

    def vouch(d, carry):
        pl.semaphore_signal(entered, inc=1, device_id=(r, tm_at(d)), device_id_type=MESH)
        return carry

    lax.fori_loop(1, 8, vouch, 0)

    prior_copy.wait()
    ptmp[...] = group_transpose(prior[...])
    for i in range(8):
        psend[i] = ptmp[:, i, :]
    sig[m] = psend[m]

    jac_copy.wait()
    pl.semaphore_wait(entered, 7)

    def send_prior(d, carry):
        t = tm_at(d)
        pltpu.make_async_remote_copy(
            src_ref=psend.at[t], dst_ref=sig.at[m], send_sem=ps_sem, recv_sem=p_sem,
            device_id=(r, t), device_id_type=MESH,
        ).start()
        return carry

    lax.fori_loop(1, 8, send_prior, 0)
    own = m
    lane = iota((1, 128), 1)
    lanes = iota((16, 128), 1) >> 4

    def deliver(g, carry):
        to = [region_at(g // 4 + 2 * k, g % 4 + 2 * k) for k in range(2)]
        which = jnp.concatenate(
            [jnp.where(iota((48, 768), 0) + t * 48 == slots[...], 1.0, 0.0) for t in to], axis=0
        ).astype(BF16)
        meta = lax.dot_general(metas[...], which, NT_DIMS, preferred_element_type=F32)
        rho_slot[...] = lax.dot_general(
            meta.astype(BF16), jnp.where(iota((16, 128), 0) == 4, 1.0, 0.0).astype(BF16), TN_DIMS,
            preferred_element_type=F32,
        ).astype(I32)
        meta = jnp.concatenate([meta, jnp.zeros((16, 32), F32)], axis=1)
        for k in range(2):
            part = meta if k == 0 else pltpu.roll(meta, 128 - 48, 1)
            msend[g * 2 + k, 0:1, :] = jnp.where(
                lane < 64, part[0:1] * 64.0 + part[1:2], pltpu.roll(part[2:3], 64, 1)
            )
            msend[g * 2 + k, 1:2, :] = part[2:3] * part[3:4]
        for l in range(0, 2048, 256):
            picked[:, l : l + 256] = dot(which, jac[:, l : l + 256])
        for k in range(2):

            def turn(i, carry, k=k):
                rows = pl.ds(pl.multiple_of(k * 48 + i * 16, 16), 16)
                out = pl.ds(pl.multiple_of(i * 16, 16), 16)
                rho = rho_slot[rows, :]
                parts = [picked[rows, l * 128 : (l + 1) * 128] for l in range(16)]
                for s in (1, 2, 4, 8):
                    bit = (rho & s) != 0
                    parts = [jnp.where(bit, parts[(l - s) % 16], parts[l]) for l in range(16)]
                for half in range(2):
                    v = parts[half * 8 : half * 8 + 8]
                    for s in (1, 2, 4):
                        bit = (lanes & s) != 0
                        new = list(v)
                        for n in range(8):
                            if n & s == 0:
                                new[n] = jnp.where(bit, pltpu.roll(v[n + s], 16 * s, 1), v[n])
                                new[n + s] = jnp.where(bit, v[n + s], pltpu.roll(v[n], 128 - 16 * s, 1))
                        v = new
                    for n in range(8):
                        xs[g * 16 + k * 8 + n, out, half * 128 : (half + 1) * 128] = v[n].astype(BF16)
                return carry

            for i in range(3):
                turn(i, 0)

        def send(k, d):
            t = tm_at((3 * d + 4 * k) % 8)
            here = g * 16 + k * 8 + m
            pltpu.make_async_remote_copy(
                src_ref=msend.at[g * 2 + k], dst_ref=mrecv.at[here], send_sem=ms_sem, recv_sem=m_sem.at[g],
                device_id=(to[k], t), device_id_type=MESH,
            ).start()
            pltpu.make_async_remote_copy(
                src_ref=xs.at[g * 16 + k * 8 + t], dst_ref=rbuf.at[here], send_sem=s_sem, recv_sem=r_sem.at[g],
                device_id=(to[k], t), device_id_type=MESH,
            ).start()

        def send_two(d, carry):
            send(0, d)
            send(1, d)
            return carry

        @pl.when(g > 0)
        def _():
            send(0, 0)

        send(1, 0)
        lax.fori_loop(1, 8, send_two, 0)
        return carry

    lax.fori_loop(0, 8, deliver, 0)
    local_rows = pltpu.make_async_copy(xs.at[own], rbuf.at[own], r_sem.at[0])
    local_meta = pltpu.make_async_copy(msend.at[0], mrecv.at[own], m_sem.at[0])
    local_rows.start()
    local_meta.start()

    factor_copy.wait()
    product = lax.dot_general(factor[...], factor[...], NT_DIMS, precision=HIGH, preferred_element_type=F32)
    for ref, value in ((cov, product), (factor_t, jnp.transpose(factor[...]))):
        ref[0:448, :] = value.astype(BF16)
        ref[448:896, :] = (value - value.astype(BF16).astype(F32)).astype(BF16)
    oi = iota((768, 768), 0)
    order[...] = jnp.where(iota((768, 768), 1) == (oi & 15) * 48 + (oi >> 4), 1.0, 0.0).astype(BF16)

    lane_lag = iota((16, 256), 1) >> 4

    def receive(g, carry):
        batch = pl.ds(g * 16, 16)
        pltpu.make_async_copy(mrecv.at[batch], mrecv.at[batch], m_sem.at[g]).wait()
        pltpu.make_async_copy(rbuf.at[batch], rbuf.at[batch], r_sem.at[g]).wait()
        rows = dot(order[...], rbuf[batch].reshape(768, 256))
        rho = mrecv[batch, 0, :].astype(I32) & 15
        for k in range(48):
            tile = rows[k * 16 : k * 16 + 16]
            later = lane_lag < rho[:, k : k + 1]
            at = pl.ds(pl.multiple_of((k % 6) * 128 + g * 16, 16), 16)
            jw[k // 6, at, 0:256] = jnp.where(later, 0.0, tile).astype(BF16)
            jw[k // 6, at, 256:512] = jnp.where(later, tile, 0.0).astype(BF16)
        return carry

    lax.fori_loop(0, 8, receive, 0)

    first = jnp.transpose(mrecv[:, 0, :])
    second = jnp.transpose(mrecv[:, 1, :])
    code = first[0:48].astype(I32)
    key[...] = ((code & 63) >> 4) * 8 + (code >> 6)
    wgt[...] = first[64:112]
    wy[...] = second[0:48]
    pltpu.make_async_copy(sig.at[pl.ds(0, 7)], sig.at[pl.ds(0, 7)], p_sem).wait()

    rows24 = iota((24, 128), 0)

    def spread(values, ready):
        def one(w, carry):
            cols = []
            for j in range(6):
                at = pl.ds(w * 6 + j, 1)
                cols.append(jnp.where(rows24 == key[at, :], values[at, :], 0.0))
            out = dot(split(jnp.concatenate(cols, axis=1)), jw[w])
            out = out[:24] + out[24:]
            for a in range(4):
                for h in range(2 if a < 3 else 1):
                    val = None
                    if a < 3:
                        val = out[8 * a : 8 * a + 8, h * 128 : h * 128 + 128]
                    if a > 0:
                        more = out[8 * a - 8 : 8 * a, 256 + h * 128 : 384 + h * 128]
                        val = more if val is None else val + more
                    ss[w * 7 + 2 * a + h] = val
            return carry

        for half in range(2):
            ready(half)
            [one(w, 0) for w in range(half * 4, half * 4 + 4)]
        return group_transpose(ss[...]).reshape(448, 128) * sig[...].reshape(448, 128)

    def observe(g_field, phase):
        h_field = sig[...].reshape(448, 128) * in_time(cov, g_field)
        ss[...] = group_transpose(h_field.reshape(56, 8, 128))

        def one(w, carry):
            rows = []
            zero = jnp.zeros((8, 128), F32)
            for a in range(3):
                cells = [ss[w * 7 + 2 * a + h] for h in range(2)]
                for h in range(2):
                    cells.append(ss[w * 7 + 2 * a + 2 + h] if 2 * a + 2 + h < 7 else zero)
                rows.append(jnp.concatenate(cells, axis=1))
            if phase == 0:
                turned = jnp.transpose(jw[w])
                jwt[w] = turned
            else:
                turned = jwt[w]
            v = dot(split(jnp.concatenate(rows, axis=0)), turned)
            v = v[:24] + v[24:]
            for j in range(6):
                uval[phase, pl.ds(w * 6 + j, 1), :] = jnp.sum(
                    jnp.where(rows24 == key[pl.ds(w * 6 + j, 1), :], v[:, j * 128 : (j + 1) * 128], 0.0),
                    axis=0, keepdims=True,
                )
            return carry

        for half in range(2):
            [one(w, 0) for w in range(half * 4, half * 4 + 4)]
            mine = uval.at[phase, pl.ds(half * 24, 24)]

            def send_values(d, carry, half=half, mine=mine):
                t = tm_at(d)
                pltpu.make_async_remote_copy(
                    src_ref=mine, dst_ref=ubuf.at[phase, half, m],
                    send_sem=us_sem.at[phase, half], recv_sem=u_sem.at[phase, half],
                    device_id=(r, t), device_id_type=MESH,
                ).start()
                return carry

            for d in range(1, 8):
                send_values(d, 0)
            ubuf[phase, half, m] = uval[phase, half * 24 : half * 24 + 24, :]

    def collect(phase):
        def ready(half):
            seven = ubuf.at[phase, half, pl.ds(0, 7)]
            pltpu.make_async_copy(seven, seven, u_sem.at[phase, half]).wait()
            total = ubuf[phase, half, 0]
            for i in range(1, 8):
                total = total + ubuf[phase, half, i]
            rows = slice(half * 24, half * 24 + 24)
            weighted = wgt[rows, :] * total
            vec[phase, rows, :] = weighted
            if phase == 0:
                terms = (wy[rows, :] * total, weighted * total)
            else:
                terms = (vec[0, rows, :] * total, weighted * total)
            for i, term in enumerate(terms):
                term = jnp.sum(term, axis=0, keepdims=True)
                at = slice(2 * phase + i, 2 * phase + i + 1)
                scal[at, :] = term if half == 0 else scal[at, :] + term
            if phase == 1 and half == 1:
                send_sums()

        return ready

    def send_field(k):
        fsend[k] = in_time(factor_t, gs[k]).reshape(8, 56, 128)

        def send(d, carry):
            t = tm_at(d)
            pltpu.make_async_remote_copy(
                src_ref=fsend.at[k, t], dst_ref=fbuf.at[k, m], send_sem=fs_sem.at[k], recv_sem=f_sem.at[k],
                device_id=(r, t), device_id_type=MESH,
            ).start()
            return carry

        for d in range(1, 8):
            send(d, 0)
        fbuf[k, m] = fsend[k, m]

    def wait_field(k):
        seven = fbuf.at[k, pl.ds(0, 7)]
        pltpu.make_async_copy(seven, seven, f_sem.at[k]).wait()

    def send_sums():
        scal_in[r] = scal[...]
        for i in range(1, 16):
            pltpu.make_async_remote_copy(
                src_ref=scal, dst_ref=scal_in.at[r], send_sem=cs_sem, recv_sem=c_sem,
                device_id=(region_at(i // 4, i % 4), m), device_id_type=MESH,
            ).start()

    scal[4:8, :] = jnp.zeros((4, 128), F32)
    gs[0] = spread(wy, lambda half: None)
    observe(gs[0], 0)
    send_field(0)
    gs[1] = spread(vec.at[0], collect(0))
    observe(gs[1], 1)
    send_field(1)
    gs[2] = spread(vec.at[1], collect(1))
    send_field(2)

    fifteen = scal_in.at[pl.ds(0, 15)]
    pltpu.make_async_copy(fifteen, fifteen, c_sem).wait()
    sums = scal_in[0]
    for i in range(1, 16):
        sums = sums + scal_in[i]
    sums = jnp.sum(sums, axis=1, keepdims=True)
    g00, g01, g11, g12 = (sums[i : i + 1, :] for i in range(4))
    a0 = g00 / (g00 + g01)
    rr1 = (1 - a0) * (1 - a0) * g00 - 2 * a0 * (1 - a0) * g01 + a0 * a0 * g11
    p, q = 1 - a0 + rr1 / g00, -a0
    a1 = rr1 / (p * p * g00 + p * (p + 2 * q) * g01 + q * (2 * p + q) * g11 + q * q * g12)
    wait_field(0)
    wait_field(1)
    for i in range(8):
        ptmp[:, i, :] = (a0 + a1 * p) * fbuf[0, i] + a1 * q * fbuf[1, i]
    x_out[...] = group_transpose(ptmp[...])
    for i in range(8):
        fbuf[0, i] = (1 - a0 - a1 * p) * fbuf[0, i] - (a0 + a1 * (p + q)) * fbuf[1, i]
    wait_field(2)
    for i in range(8):
        ptmp[:, i, :] = fbuf[0, i] - a1 * q * fbuf[2, i]
    r_out[...] = group_transpose(ptmp[...])

    all_rows, all_meta = xs.at[pl.ds(0, 127)], mrecv.at[pl.ds(0, 127)]
    pltpu.make_async_copy(all_rows, all_rows, s_sem).wait()
    pltpu.make_async_copy(all_meta, all_meta, ms_sem).wait()
    seven = sig.at[pl.ds(0, 7)]
    pltpu.make_async_copy(seven, seven, ps_sem).wait()
    for phase in range(2):
        for half in range(2):
            seven = ubuf.at[phase, half, pl.ds(0, 7)]
            pltpu.make_async_copy(seven, seven, us_sem.at[phase, half]).wait()
    pltpu.make_async_copy(fifteen, fifteen, cs_sem).wait()
    for k in range(3):
        seven = fbuf.at[k, pl.ds(0, 7)]
        pltpu.make_async_copy(seven, seven, fs_sem.at[k]).wait()


def hand_on(x_in, r_in, x_out, r_out):
    x_out[...] = x_in[...]
    r_out[...] = r_in[...]


def local(jacobian, foot_block, foot_time, obs_weight, misfit, kept_list, kept_count, prior_std, time_factor):
    field = jax.ShapeDtypeStruct(prior_std.shape, F32)
    vmem = pl.BlockSpec(memory_space=pltpu.VMEM)
    hbm = pl.BlockSpec(memory_space=pltpu.HBM)
    dma = pltpu.SemaphoreType.DMA
    fields = pl.pallas_call(
        kernel,
        out_shape=(field, field),
        in_specs=[vmem] * 5 + [pl.BlockSpec(memory_space=pltpu.SMEM)] + [hbm] * 3,
        out_specs=(vmem, vmem),
        scratch_shapes=[
            pltpu.VMEM((768, 2048), BF16),
            pltpu.VMEM((56, 8, 128), F32),
            pltpu.VMEM((448, 448), F32),
            pltpu.VMEM((896, 448), BF16),
            pltpu.VMEM((1, 768), I32),
            pltpu.VMEM((16, 768), BF16),
            pltpu.VMEM((768, 768), BF16),
            pltpu.VMEM((96, 128), I32),
            pltpu.VMEM((96, 2048), F32),
            pltpu.VMEM((128, 48, 256), BF16),
            pltpu.VMEM((128, 48, 256), BF16),
            pltpu.VMEM((16, 2, 128), F32),
            pltpu.VMEM((128, 2, 128), F32),
            pltpu.VMEM((8, 768, 512), BF16),
            pltpu.VMEM((8, 512, 768), BF16),
            pltpu.VMEM((8, 56, 128), F32),
            pltpu.VMEM((8, 56, 128), F32),
            pltpu.VMEM((896, 448), BF16),
            pltpu.VMEM((48, 128), I32),
            pltpu.VMEM((48, 128), F32),
            pltpu.VMEM((48, 128), F32),
            pltpu.VMEM((2, 48, 128), F32),
            pltpu.VMEM((2, 2, 8, 24, 128), F32),
            pltpu.VMEM((2, 48, 128), F32),
            pltpu.VMEM((56, 8, 128), F32),
            pltpu.VMEM((3, 448, 128), F32),
            pltpu.VMEM((8, 128), F32),
            pltpu.VMEM((16, 8, 128), F32),
            pltpu.VMEM((3, 8, 56, 128), F32),
            pltpu.VMEM((3, 8, 56, 128), F32),
            pltpu.VMEM((56, 8, 128), F32),
            pltpu.SemaphoreType.REGULAR, dma((3,)), dma, dma, dma((8,)), dma((8,)), dma, dma, dma((2, 2)), dma((2, 2)), dma, dma, dma((3,)), dma((3,)),
        ],
        compiler_params=pltpu.CompilerParams(
            collective_id=0, has_side_effects=True, vmem_limit_bytes=60 * 2**20
        ),
    )(foot_block, foot_time, obs_weight, misfit, kept_list, kept_count, jacobian, prior_std, time_factor)
    return pl.pallas_call(
        hand_on, out_shape=(field, field), in_specs=[vmem, vmem], out_specs=(vmem, vmem)
    )(*fields)


def solution(mesh):
    rows = P(("region", "tm"))
    return jax.shard_map(
        local,
        mesh=mesh,
        in_specs=(
            P(("region", "tm"), None), rows, rows, rows, rows, rows, rows, P("tm", "region", None), P(),
        ),
        out_specs=(P("tm", "region", None), P("tm", "region", None)),
        check_vma=False,
    )
```
